32 devices in a mesh: groups: 2 (over x), resp: 4 (over z), expert: 4 (over y, core).
Axes of the slice: x: 2, y: 2, z: 4, core: 2. Of those that a mesh axis runs over, the one named last changes fastest.
Arguments:
- x_prompt: bfloat16 [8, 8, 4096], P(('groups', 'expert'), 'resp'), parts along dimension 0, may hold values from -6 to 6
- x_resp: bfloat16 [8, 4, 4, 4096], P(('groups', 'expert'), 'resp'), parts along dimension 0, may hold values from -6 to 6
- prompt_cot: bfloat16 [8, 4, 8, 4096], P(('groups', 'expert'), 'resp'), parts along dimension 0, may hold values from -6 to 6
- resp_cot: bfloat16 [8, 4, 4, 4096], P(('groups', 'expert'), 'resp'), parts along dimension 0, may hold values from -24 to 24
- route_prompt: int32 [8, 8, 2], P(('groups', 'expert'), 'resp'), parts along dimension 0, may hold values from 0 to 3, all different within a row; in each aligned block of 2 rows (0 to 1, 2 to 3, ..., all dimensions but the last counted through in order) at most 2 rows name the same one
- route_resp: int32 [8, 4, 4, 2], P(('groups', 'expert'), 'resp'), parts along dimension 0, may hold values from 0 to 3, all different within a row; in each aligned block of 4 rows (0 to 3, 4 to 7, ..., all dimensions but the last counted through in order) at most 2 rows name the same one
- weight_prompt: float32 [8, 8, 2], P(('groups', 'expert'), 'resp'), parts along dimension 0, may hold values from 0.03 to 0.4
- weight_resp: float32 [8, 4, 4, 2], P(('groups', 'expert'), 'resp'), parts along dimension 0, may hold values from 0.03 to 0.4
- w_gate: bfloat16 [4, 1536, 4096], P('expert', 'resp'), may hold values from -0.09375 to 0.09375
- w_up: bfloat16 [4, 1536, 4096], P('expert', 'resp'), may hold values from -0.09375 to 0.09375
- w_down: bfloat16 [4, 1536, 4096], P('expert', 'resp'), may hold values from -0.15625 to 0.15625
Outputs:
- grad_prompt: bfloat16 [8, 8, 4096], P(('groups', 'expert'), 'resp'), parts along dimension 0
- grad_resp: bfloat16 [8, 4, 4, 4096], P(('groups', 'expert'), 'resp'), parts along dimension 0
- grad_gate: bfloat16 [8, 1536, 4096], P(('groups', 'expert'), 'resp'), parts along dimension 0
- grad_up: bfloat16 [8, 1536, 4096], P(('groups', 'expert'), 'resp'), parts along dimension 0
- grad_down: bfloat16 [8, 1536, 4096], P(('groups', 'expert'), 'resp'), parts along dimension 0
The draws below stay inside these ranges and needn't reach their ends.
There are 2 independent parts, one for each index of `groups`. The reference program is written for one: setup_inputs(seed, part) draws one part's arguments, and reference() takes and returns one part's arrays. A program takes and returns all parts, laid end to end along the dimension named above; an argument that names none is the same for every part. Nothing has to cross between parts.
Inputs may be any that keep to these rules, and one draw needn't show every extreme that they name: `route_prompt`: each row names 2 different experts; within each aligned block of 2 prompt rows (the rows of one device) no expert is named by more than 2 rows. `route_resp`: each token names 2 different experts; within the 4 tokens of one response no expert is named by more than 2 tokens, and some expert reaches 2.
All inputs are finite; a program needn't handle non-finite values.
Results may differ from the reference program's by a relative error of at most 0.019.
Values may be sent and summed in bfloat16 or wider, within the bound.
No kernel may reach another device: no remote copies, remote signals or barrier semaphores. Data moves between devices by JAX's collectives and lax.ppermute only.
A program may use at most 128 MiB of HBM per device.

```python
import math
import jax
import jax.numpy as jnp
import numpy as np
from jax import lax

D = 4096
H = 1536
PROMPT_DEV = 2
LEN = 4
RESP_DEV = 1
EXPERTS = 4
TOP = 2
PROMPTS = 4
PROMPT = 8
RESP = 4
CAP_P = 2
CAP_R = 2
SLOTS = 4
N_RESP = 4
N_EXPERT = 4


def raised(entries, own_key, source, target, blocks, factor):
    def block_of(position):
        return (jnp.arange(entries.shape[position]) // (entries.shape[position] // blocks)).reshape((-1,) + (1,) * (entries.ndim - 1 - position))

    near = jax.random.permutation(own_key, blocks)[block_of(target)]
    other_side = (block_of(target) + blocks // 2) % blocks
    return jnp.where((block_of(source) == near) | (block_of(source) == other_side), factor * entries, entries)


def block_scale(rng, extent, shards, least, high):
    factor_of = 1.0
    for position, blocks in shards:
        draws = jax.random.uniform(jax.random.fold_in(jax.random.fold_in(rng, 6), position), (blocks,), jnp.float32, least / len(shards), high / len(shards))
        factor_of = factor_of * jnp.repeat(jnp.exp(draws), extent[position] // blocks).reshape((-1,) + (1,) * (len(extent) - 1 - position))
    return factor_of


def assign_block(key, own, number, rows, amount, top, most, lean):
    order = jax.random.permutation(key, amount)
    crowded, common = portions_of(amount, rows * top, most, lean, True), portions_of(amount, rows * top, most, lean, False)
    places = jnp.arange(amount)

    def named(lengths, offset_by):
        used = int((lengths > 0).sum())
        fixed = max(1, used // 4)
        passed = fixed + (places - fixed + offset_by * (used - fixed)) % max(1, amount - fixed)
        return jnp.zeros((amount,), jnp.int32).at[order[jnp.where(places < fixed, places, passed)]].set(jnp.asarray(lengths, jnp.int32))

    lengths = jnp.where(number % 4 == 0, named(crowded, number // 4), named(common, number - number // 4 - 1))
    mixed = jax.random.permutation(jax.random.fold_in(own, 3), amount)
    giver, receiver = mixed[0:amount // 2 * 2:2], mixed[1:amount // 2 * 2:2]
    margin = jnp.minimum(lengths[giver] - 1, most - lengths[receiver]) // 2
    margin = jnp.where((giver == order[0]) | (receiver == order[0]) | (lengths[receiver] == 0), 0, jnp.maximum(margin, 0))
    passed = jax.random.randint(jax.random.fold_in(own, 4), (amount // 2,), 0, 1 << 20) % (margin + 1)
    lengths = lengths.at[giver].add(-passed).at[receiver].add(passed)
    items = jnp.searchsorted(jnp.cumsum(lengths), jnp.arange(rows * top), side="right").astype(jnp.int32)
    table = items.reshape(top, rows).T
    table = table[jax.random.permutation(jax.random.fold_in(own, 1), rows)]
    offset_by = jax.random.randint(jax.random.fold_in(own, 2), (rows, 1), 0, top)
    return jnp.take_along_axis(table, (jnp.arange(top)[None, :] + offset_by) % top, axis=1)


def portions_of(count, total, reach, lean, full):
    loads = [(1 << 20) // math.isqrt(rank ** lean) + 1 for rank in range(1, count + 1)]
    largest = reach if full else min(reach, max(-(-total // count), total * loads[0] // sum(loads)))
    least = 1 if total - largest >= count - 1 else 0
    given, rest = [largest] + [least] * (count - 1), total - largest - least * (count - 1)
    while rest > 0:
        movable = [i for i in range(1, count) if given[i] < largest] or [i for i in range(1, count) if given[i] < reach]
        whole, budget = sum([loads[i] for i in movable]), rest
        for i in movable:
            more = min(reach - given[i], max(1, budget * loads[i] // whole), rest)
            given[i] = given[i] + more
            rest = rest - more
    return np.array(given)


def noise(own_key, dims, width, bound, pieces=(), kind=jnp.bfloat16):
    array = width * jax.random.normal(own_key, dims, jnp.float32)
    if pieces:
        array = array * block_scale(own_key, dims, pieces, -0.22, 0.18)
    return jnp.clip(array, -bound, bound).astype(kind)


def gaussian_with(rng, extent, deviation, reach, pieces, heavy, kind=jnp.bfloat16):
    entries = deviation * jax.random.normal(rng, extent, jnp.float32)
    if pieces:
        entries = entries * block_scale(rng, extent, pieces, -0.22, 0.18)
    return jnp.clip(raised(entries, jax.random.fold_in(rng, 3), *heavy), -reach, reach).astype(kind)


def setup_inputs(seed: int = 0, part: int = 0) -> dict:
    keys = jax.random.split(jax.random.key(seed), 12)
    part_keys = jax.random.split(jax.random.fold_in(keys[11], part), 12)
    x_prompt = noise(part_keys[0], (PROMPTS, PROMPT, D), 1.0, 6.0, ((0, 4), (1, 4)))
    x_resp = noise(part_keys[1], (PROMPTS, RESP, LEN, D), 1.0, 6.0, ((0, 4), (1, 4)))
    prompt_cot = gaussian_with(part_keys[2], (PROMPTS, RESP, PROMPT, D), 1.0, 6.0, ((0, 4), (1, 4)), (1, 2, 4, 2.0))
    resp_cot = noise(part_keys[3], (PROMPTS, RESP, LEN, D), 4.0, 24.0, ((0, 4), (1, 4)))
    route_prompt_keys = jax.random.split(jax.random.fold_in(part_keys[4], 1), PROMPTS * PROMPT // PROMPT_DEV)
    route_prompt_turns = jax.random.permutation(jax.random.fold_in(part_keys[4], 3), PROMPTS * PROMPT // PROMPT_DEV)
    route_prompt = jax.vmap(lambda own, number: assign_block(jax.random.fold_in(part_keys[4], 2), own, number, PROMPT_DEV, EXPERTS, TOP, CAP_P, 2))(route_prompt_keys, route_prompt_turns).reshape((PROMPTS, PROMPT, TOP))
    route_resp_keys = jax.random.split(jax.random.fold_in(part_keys[5], 1), PROMPTS * RESP * LEN // LEN)
    route_resp_turns = jax.random.permutation(jax.random.fold_in(part_keys[5], 3), PROMPTS * RESP * LEN // LEN)
    route_resp = jax.vmap(lambda own, number: assign_block(jax.random.fold_in(part_keys[5], 2), own, number, LEN, EXPERTS, TOP, CAP_R, 2))(route_resp_keys, route_resp_turns).reshape((PROMPTS, RESP, LEN, TOP))
    weight_prompt = jnp.clip(jnp.exp(math.log(0.4) - 2.5902672 * jax.random.uniform(part_keys[6], (PROMPTS, PROMPT, TOP), jnp.float32) ** block_scale(part_keys[6], (PROMPTS, PROMPT, TOP), ((0, 4), (1, 4)), -0.2, 0.2)), 0.03, 0.4)
    weight_resp = jnp.clip(jnp.exp(math.log(0.4) - 2.5902672 * jax.random.uniform(part_keys[7], (PROMPTS, RESP, LEN, TOP), jnp.float32) ** block_scale(part_keys[7], (PROMPTS, RESP, LEN, TOP), ((0, 4), (1, 4)), -0.2, 0.2)), 0.03, 0.4)
    w_gate = noise(keys[8], (EXPERTS, H, D), D ** -0.5, 0.09375, ((0, 4), (1, 4)))
    w_up = noise(keys[9], (EXPERTS, H, D), D ** -0.5, 0.09375, ((0, 4), (1, 4)))
    w_down = noise(keys[10], (EXPERTS, H, D), H ** -0.5, 0.15625, ((0, 4), (1, 4)))
    return {"x_prompt": x_prompt, "x_resp": x_resp, "prompt_cot": prompt_cot, "resp_cot": resp_cot, "route_prompt": route_prompt, "route_resp": route_resp, "weight_prompt": weight_prompt, "weight_resp": weight_resp, "w_gate": w_gate, "w_up": w_up, "w_down": w_down}


def route_slots(expert_ids, experts):
    onehot = (expert_ids[..., None] == jnp.arange(experts, dtype=jnp.int32)).astype(jnp.int32)
    member = jnp.sum(onehot, axis=-2)
    before = jnp.cumsum(member, axis=-2) - member
    return jnp.sum(onehot * before[..., None, :], axis=-1)


def reference(x_prompt, x_resp, prompt_cot, resp_cot, route_prompt, route_resp, weight_prompt, weight_resp, w_gate, w_up, w_down):
    dy_prompt = jnp.sum(prompt_cot.astype(jnp.float32), axis=1).astype(jnp.bfloat16)
    prompt_rows = PROMPTS * PROMPT
    resp_rows = PROMPTS * RESP * LEN
    slot_prompt = route_slots(route_prompt.reshape(PROMPTS, N_RESP, PROMPT_DEV, TOP), EXPERTS)
    prompt_index = jnp.arange(PROMPTS, dtype=jnp.int32)
    holder = jnp.arange(N_RESP, dtype=jnp.int32)
    source = holder[None, :] * N_EXPERT + prompt_index[:, None]
    place_prompt = (source[:, :, None, None] * SLOTS + slot_prompt).reshape(prompt_rows, TOP)
    slot_resp = route_slots(route_resp, EXPERTS)
    response = jnp.arange(RESP, dtype=jnp.int32)
    source_resp = (response // RESP_DEV)[None, :] * N_EXPERT + prompt_index[:, None]
    offset = CAP_P + (response % RESP_DEV) * CAP_R
    place_resp = (source_resp[:, :, None, None] * SLOTS + offset[None, :, None, None] + slot_resp).reshape(resp_rows, TOP)
    tokens = prompt_rows + resp_rows
    expert_ids = jnp.concatenate([route_prompt.reshape(prompt_rows, TOP), route_resp.reshape(resp_rows, TOP)], axis=0)
    placement = jnp.concatenate([place_prompt, place_resp], axis=0).astype(jnp.int32)
    router = jnp.concatenate([weight_prompt.reshape(prompt_rows, TOP), weight_resp.reshape(resp_rows, TOP)], axis=0)
    inputs = jnp.concatenate([x_prompt.reshape(prompt_rows, D), x_resp.reshape(resp_rows, D)], axis=0)
    outgrad = jnp.concatenate([dy_prompt.reshape(prompt_rows, D), resp_cot.reshape(resp_rows, D)], axis=0)
    routed = (router[:, :, None] * outgrad[:, None, :].astype(jnp.float32)).astype(jnp.bfloat16)
    routed = routed.reshape(tokens * TOP, D)
    rows = N_RESP * N_EXPERT * SLOTS
    token_index = jnp.broadcast_to(jnp.arange(tokens, dtype=jnp.int32)[:, None], (tokens, TOP))
    route_index = jnp.arange(tokens * TOP, dtype=jnp.int32).reshape(tokens, TOP)
    token_table = jnp.full((EXPERTS, rows), tokens, jnp.int32).at[expert_ids, placement].set(token_index)
    route_table = jnp.full((EXPERTS, rows), tokens * TOP, jnp.int32).at[expert_ids, placement].set(route_index)
    inputs_pad = jnp.concatenate([inputs, jnp.zeros((1, D), jnp.bfloat16)], axis=0)
    routed_pad = jnp.concatenate([routed, jnp.zeros((1, D), jnp.bfloat16)], axis=0)
    groups = H // N_RESP

    def one_expert(operands):
        token_rows, route_rows, gate_w, up_w, down_w = operands
        rows_in = inputs_pad[token_rows]
        rows_grad = routed_pad[route_rows]
        gate = jnp.dot(rows_in, gate_w.T, preferred_element_type=jnp.float32)
        upward = jnp.dot(rows_in, up_w.T, preferred_element_type=jnp.float32)
        sigma = jax.nn.sigmoid(gate)
        active = gate * sigma
        hidden = (active * upward).astype(jnp.bfloat16)
        hidden_grad = jnp.dot(rows_grad, down_w.T, preferred_element_type=jnp.float32)
        gate_grad = (hidden_grad * upward * sigma * (1.0 + gate * (1.0 - sigma))).astype(jnp.bfloat16)
        upward_grad = (hidden_grad * active).astype(jnp.bfloat16)
        grad_g = jnp.dot(gate_grad.T, rows_in, preferred_element_type=jnp.float32).astype(jnp.bfloat16)
        grad_u = jnp.dot(upward_grad.T, rows_in, preferred_element_type=jnp.float32).astype(jnp.bfloat16)
        grad_d = jnp.dot(hidden.T, rows_grad, preferred_element_type=jnp.float32).astype(jnp.bfloat16)
        gate_three = gate_grad.astype(jnp.float32).reshape(rows, N_RESP, groups)
        upward_three = upward_grad.astype(jnp.float32).reshape(rows, N_RESP, groups)
        gate_wthree = gate_w.astype(jnp.float32).reshape(N_RESP, groups, D)
        up_wthree = up_w.astype(jnp.float32).reshape(N_RESP, groups, D)
        parts = jnp.einsum('mgh,ghd->gmd', gate_three, gate_wthree, precision=lax.Precision.HIGHEST)
        parts = parts + jnp.einsum('mgh,ghd->gmd', upward_three, up_wthree, precision=lax.Precision.HIGHEST)
        rounded = lax.optimization_barrier(parts.astype(jnp.bfloat16))
        route_dx = jnp.sum(rounded.astype(jnp.float32), axis=0).astype(jnp.bfloat16)
        return (grad_g, grad_u, grad_d, route_dx)

    grad_gate, grad_up, grad_down, route_dx = lax.map(one_expert, (token_table, route_table, w_gate, w_up, w_down))
    per_route = route_dx[expert_ids, placement]
    token_grad = jnp.sum(per_route.astype(jnp.float32), axis=1).astype(jnp.bfloat16)
    grad_prompt = token_grad[:prompt_rows].reshape(PROMPTS, PROMPT, D)
    grad_resp = token_grad[prompt_rows:].reshape(PROMPTS, RESP, LEN, D)
    return (grad_prompt, grad_resp, grad_gate, grad_up, grad_down)
```

```python
import functools

import jax
import jax.numpy as jnp
from jax import lax
from jax.experimental import pallas as pl
from jax.experimental.pallas import tpu as pltpu
from jax.sharding import PartitionSpec as P

LANES = 128
VMEM = pl.BlockSpec(memory_space=pltpu.VMEM)
SMEM = pl.BlockSpec(memory_space=pltpu.SMEM)


def params(mib):
    return pltpu.CompilerParams(vmem_limit_bytes=mib * 2**20)


def contract_last(left, right):
    return lax.dot_general(
        left, right, (((1,), (1,)), ((), ())), preferred_element_type=jnp.float32
    )


def contract_first(left, right):
    return lax.dot_general(
        left, right, (((0,), (0,)), ((), ())), preferred_element_type=jnp.float32
    )


def along(axis, size, by):
    return lambda value: lax.ppermute(value, axis, [(i, (i + by) % size) for i in range(size)])


def other_core(value, size):
    return lax.ppermute(value, "expert", [(i, i ^ 1) for i in range(size)])


def router_row(routes, weights, row, top, experts):
    lane = lax.broadcasted_iota(jnp.int32, (1, LANES), 1)
    dense = jnp.zeros((1, LANES), jnp.float32)
    for k in range(top):
        dense = dense + jnp.where(lane % experts == routes(row, k), weights(row, k), 0.0)
    high = dense.astype(jnp.bfloat16).astype(jnp.float32)
    middle = (dense - high).astype(jnp.bfloat16).astype(jnp.float32)
    low = dense - high - middle
    part = lane // experts
    return jnp.where(part == 0, high, jnp.where(part == 1, middle, jnp.where(part == 2, low, 0.0)))


def prepare_kernel(experts, x_prompt, x_resp, prompt_cot, resp_cot, route_p, route_r, weight_p, weight_r, sent_r, sent_p, *shares):
    width = x_prompt.shape[-1]
    rows_p = x_prompt.shape[1]
    responses, length = x_resp.shape[1:3]
    top = route_p.shape[-2]
    x = [x_resp[0, i].astype(jnp.float32) for i in range(responses)]
    dy = [resp_cot[0, i].astype(jnp.float32) for i in range(responses)]
    sent_r[:, :width] = jnp.concatenate(x + dy, axis=0).astype(jnp.bfloat16)
    rows = [
        router_row(lambda t, k: route_r[0, i, k, t], lambda t, k: weight_r[0, i, k, t], t, top, experts)
        for i in range(responses)
        for t in range(length)
    ]
    rows.append(jnp.zeros((len(rows), LANES), jnp.float32))
    sent_r[:, width:] = jnp.concatenate(rows, axis=0).astype(jnp.bfloat16)
    sent_p[:, :width] = x_prompt[0]
    rows = [
        router_row(lambda t, k: route_p[0, k, t], lambda t, k: weight_p[0, k, t], t, top, experts)
        for t in range(rows_p)
    ]
    sent_p[:, width:] = jnp.concatenate(rows, axis=0).astype(jnp.bfloat16)
    cot = prompt_cot[0, 0].astype(jnp.float32)
    for i in range(1, responses):
        cot = cot + prompt_cot[0, i].astype(jnp.float32)
    rows = cot.shape[0]
    here = lax.axis_index("resp") * rows_p
    cot = pltpu.roll(cot, (rows - here) % rows, 0)
    for k, share in enumerate(shares):
        share[...] = cot[k * rows_p : (k + 1) * rows_p].astype(jnp.bfloat16)


def expert_kernel(count, spans, experts, *refs):
    width = refs[2 * count].shape[-1]
    blocks_r, blocks_p = refs[:count], refs[count : 2 * count]
    gate_w, up_w, down_w, part, rows_out, gate_out, up_out, hidden_out = refs[2 * count :]
    span_r, span_p = spans
    tails = []
    base = 0
    for block in (*blocks_r, *blocks_p):
        rows = block.shape[0]
        rows_out[base : base + rows, :] = block[:, :width]
        tails.append(block[:, width:].astype(jnp.float32))
        base += rows
    total = base
    split = sum(b.shape[0] for b in blocks_r)
    tail = jnp.concatenate(tails, axis=0)
    lane = lax.broadcasted_iota(jnp.int32, tail.shape, 1)
    mine = (lane % experts == lax.axis_index("expert")) & (lane < 3 * experts)
    router = jnp.sum(jnp.where(mine, tail, 0.0), axis=1, keepdims=True)
    values = rows_out[...]
    gate = contract_last(values, gate_w[0])
    upward = contract_last(values, up_w[0])
    wide = contract_last(values, down_w[0])

    def moved(value, up):
        top, low = value[:split], value[split:]
        by_r, by_p = (split - span_r, total - split - span_p) if up else (span_r, span_p)
        return jnp.concatenate([pltpu.roll(top, by_r, 0), pltpu.roll(low, by_p, 0)], axis=0)

    sigma = jax.nn.sigmoid(gate)
    active = gate * sigma
    hidden = router * active * upward
    hidden_grad = router * moved(wide, True)
    gate_grad = (hidden_grad * upward * sigma * (1.0 + gate * (1.0 - sigma))).astype(jnp.bfloat16)
    upward_grad = (hidden_grad * active).astype(jnp.bfloat16)
    gate_out[...] = gate_grad
    up_out[...] = upward_grad
    hidden_out[...] = moved(hidden, False).astype(jnp.bfloat16)
    tokens = part.shape[0]
    each = span_r + span_p
    slot = lax.broadcasted_iota(jnp.int32, (tokens, total), 0)
    row = lax.broadcasted_iota(jnp.int32, (tokens, total), 1)
    source, token = slot // each, slot % each
    from_r = source * (2 * span_r) + token
    from_p = split + source * (2 * span_p) + token - span_r
    chosen = (row == jnp.where(token < span_r, from_r, from_p)).astype(jnp.float32).astype(jnp.bfloat16)
    gate_grad = jnp.dot(chosen, gate_grad, preferred_element_type=jnp.float32).astype(jnp.bfloat16)
    upward_grad = jnp.dot(chosen, upward_grad, preferred_element_type=jnp.float32).astype(jnp.bfloat16)
    step = 1024 if width % 1024 == 0 else width
    for c in range(0, width, step):
        value = jnp.dot(gate_grad, gate_w[0, :, c : c + step], preferred_element_type=jnp.float32)
        value = value + jnp.dot(upward_grad, up_w[0, :, c : c + step], preferred_element_type=jnp.float32)
        part[:, c : c + step] = value.astype(jnp.bfloat16)


def body(
    x_prompt,
    x_resp,
    prompt_cot,
    resp_cot,
    route_prompt,
    route_resp,
    weight_prompt,
    weight_resp,
    w_gate,
    w_up,
    w_down,
):
    n_resp = lax.axis_size("resp")
    n_expert = lax.axis_size("expert")
    chips = n_expert // 2
    experts = n_expert * w_gate.shape[0]
    hidden_units = w_gate.shape[1]
    width = x_prompt.shape[-1]
    rows_p = x_prompt.shape[1]
    rows_r = x_resp.shape[1] * x_resp.shape[2]
    bf16 = jnp.bfloat16

    sent_r, half_p, *shares = pl.pallas_call(
        functools.partial(prepare_kernel, experts),
        out_shape=[
            jax.ShapeDtypeStruct((2 * rows_r, width + LANES), bf16),
            jax.ShapeDtypeStruct((rows_p, width + LANES), bf16),
        ]
        + [jax.ShapeDtypeStruct((rows_p, width), bf16)] * n_resp,
        in_specs=[VMEM] * 4 + [SMEM] * 4,
        out_specs=[VMEM] * (2 + n_resp),
        compiler_params=params(16),
        name="prepare",
    )(
        x_prompt,
        x_resp,
        prompt_cot,
        resp_cot,
        jnp.swapaxes(route_prompt, -1, -2),
        jnp.swapaxes(route_resp, -1, -2),
        jnp.swapaxes(weight_prompt, -1, -2),
        jnp.swapaxes(weight_resp, -1, -2),
    )

    def gather(message):
        line = jnp.concatenate([message] + [along("resp", n_resp, k)(message) for k in range(1, n_resp)], axis=0)
        near = [line] + [along("expert", n_expert, 2 * j)(line) for j in range(1, chips)]
        return near + [other_core(block, n_expert) for block in near]

    all_r = gather(sent_r)
    dy_prompt = shares[0].astype(jnp.float32)
    for k in range(1, n_resp):
        dy_prompt = dy_prompt + along("resp", n_resp, k)(shares[k]).astype(jnp.float32)
    dy_prompt = jnp.pad(dy_prompt.astype(bf16), ((0, 0), (0, LANES)))
    all_p = gather(jnp.concatenate([half_p, dy_prompt], axis=0))

    count = len(all_r)
    rows = sum(b.shape[0] for b in (*all_r, *all_p))
    tokens = rows // 2
    part, values, gate_grad, upward_grad, hidden = pl.pallas_call(
        functools.partial(expert_kernel, count, (rows_r, rows_p), experts),
        out_shape=[
            jax.ShapeDtypeStruct((tokens, width), bf16),
            jax.ShapeDtypeStruct((rows, width), bf16),
        ]
        + [jax.ShapeDtypeStruct((rows, hidden_units), bf16)] * 3,
        in_specs=[VMEM] * (2 * count + 3),
        out_specs=[VMEM] * 5,
        compiler_params=params(60),
        cost_estimate=pl.CostEstimate(flops=10 * rows * width * hidden_units, bytes_accessed=20 * 2**20, transcendentals=0),
        name="expert",
    )(*all_r, *all_p, w_gate, w_up, w_down)

    half = tokens // 2
    total = part[:half].astype(jnp.float32) + other_core(part[half:], n_expert).astype(jnp.float32)
    total = total.astype(bf16)
    block = half // chips
    line = total[:block].astype(jnp.float32)
    for j in range(1, chips):
        line = line + along("expert", n_expert, -2 * j)(total[j * block : (j + 1) * block]).astype(jnp.float32)
    line = line.astype(bf16)
    each = rows_r + rows_p
    own = line[:each].astype(jnp.float32)
    for k in range(1, n_resp):
        own = own + along("resp", n_resp, -k)(line[k * each : (k + 1) * each]).astype(jnp.float32)
    own = own.astype(bf16)

    grad_gate = contract_first(gate_grad, values).astype(bf16)[None]
    grad_up = contract_first(upward_grad, values).astype(bf16)[None]
    grad_down = contract_first(hidden, values).astype(bf16)[None]
    return (own[rows_r:][None], own[:rows_r].reshape(x_resp.shape), grad_gate, grad_up, grad_down)


def solution(mesh):
    return jax.shard_map(
        body,
        mesh=mesh,
        in_specs=(
            P(("groups", "expert"), "resp", None),
            P(("groups", "expert"), "resp", None, None),
            P(("groups", "expert"), "resp", None, None),
            P(("groups", "expert"), "resp", None, None),
            P(("groups", "expert"), "resp", None),
            P(("groups", "expert"), "resp", None, None),
            P(("groups", "expert"), "resp", None),
            P(("groups", "expert"), "resp", None, None),
            P("expert", "resp", None),
            P("expert", "resp", None),
            P("expert", "resp", None),
        ),
        out_specs=(
            P(("groups", "expert"), "resp", None),
            P(("groups", "expert"), "resp", None, None),
            P(("groups", "expert"), "resp", None),
            P(("groups", "expert"), "resp", None),
            P(("groups", "expert"), "resp", None),
        ),
        check_vma=False,
    )
```

```python
import functools

import jax
import jax.numpy as jnp
from jax import lax
from jax.experimental import pallas as pl
from jax.experimental.pallas import tpu as pltpu
from jax.sharding import PartitionSpec as P

LANES = 128
held = pltpu.with_memory_space_constraint
VMEM = pl.BlockSpec(memory_space=pltpu.VMEM)
HBM = pl.BlockSpec(memory_space=pltpu.HBM)


def params(mib):
    return pltpu.CompilerParams(vmem_limit_bytes=mib * 2**20)


def contract_last(left, right):
    return lax.dot_general(
        left, right, (((1,), (1,)), ((), ())), preferred_element_type=jnp.float32
    )


def contract_first(left, right):
    return lax.dot_general(
        left, right, (((0,), (0,)), ((), ())), preferred_element_type=jnp.float32
    )


def along(axis, size, by):
    return lambda value: lax.ppermute(value, axis, [(i, (i + by) % size) for i in range(size)])


def other_core(value, size):
    return lax.ppermute(value, "expert", [(i, i ^ 1) for i in range(size)])


def router_row(routes, weights, row, top, experts):
    lane = lax.broadcasted_iota(jnp.int32, (1, LANES), 1)
    dense = jnp.zeros((1, LANES), jnp.float32)
    for k in range(top):
        dense = dense + jnp.where(lane % experts == routes(row, k), weights(row, k), 0.0)
    high = dense.astype(jnp.bfloat16).astype(jnp.float32)
    middle = (dense - high).astype(jnp.bfloat16).astype(jnp.float32)
    low = dense - high - middle
    part = lane // experts
    return jnp.where(part == 0, high, jnp.where(part == 1, middle, jnp.where(part == 2, low, 0.0)))


def prepare_kernel(experts, *refs):
    n_in = 8
    sources, outs, scratch = refs[:n_in], refs[n_in : len(refs) - n_in - 1], refs[len(refs) - n_in - 1 : -1]
    arrived = refs[-1]
    copies = [pltpu.make_async_copy(a, b, arrived.at[i]) for i, (a, b) in enumerate(zip(sources, scratch, strict=True))]
    for copy in copies:
        copy.start()
    for copy in copies:
        copy.wait()
    x_prompt, x_resp, prompt_cot, resp_cot, route_p, route_r, weight_p, weight_r = scratch
    sent_r, sent_p = outs
    width = x_prompt.shape[-1]
    rows_p = x_prompt.shape[1]
    responses, length = x_resp.shape[1:3]
    top = route_p.shape[-1]
    x = [x_resp[0, i].astype(jnp.float32) for i in range(responses)]
    dy = [resp_cot[0, i].astype(jnp.float32) for i in range(responses)]
    sent_r[:, :width] = jnp.concatenate(x + dy, axis=0).astype(jnp.bfloat16)
    rows = [
        router_row(lambda t, k: route_r[0, i, k, t], lambda t, k: weight_r[0, i, k, t], t, top, experts)
        for i in range(responses)
        for t in range(length)
    ]
    rows.append(jnp.zeros((len(rows), LANES), jnp.float32))
    sent_r[:, width:] = jnp.concatenate(rows, axis=0).astype(jnp.bfloat16)
    cot = prompt_cot[0, 0].astype(jnp.float32)
    for i in range(1, responses):
        cot = cot + prompt_cot[0, i].astype(jnp.float32)
    prompts = cot.shape[0]
    here = lax.axis_index("resp") * rows_p
    own = jnp.concatenate([x_prompt[0].astype(jnp.float32), jnp.zeros((prompts - rows_p, width), jnp.float32)], axis=0)
    sent_p[:, :width] = jnp.concatenate([pltpu.roll(own, here, 0), cot], axis=0).astype(jnp.bfloat16)
    rows = [
        router_row(lambda t, k: route_p[0, t, k], lambda t, k: weight_p[0, t, k], t, top, experts)
        for t in range(rows_p)
    ]
    rows.append(jnp.zeros((prompts - rows_p, LANES), jnp.float32))
    own = pltpu.roll(jnp.concatenate(rows, axis=0), here, 0)
    sent_p[:, width:] = jnp.concatenate([own, jnp.zeros((prompts, LANES), jnp.float32)], axis=0).astype(jnp.bfloat16)


def expert_kernel(count, spans, experts, *refs):
    width = refs[2 * count].shape[-1]
    blocks_r, blocks_p = refs[:count], refs[count : 2 * count]
    gate_w, up_w, down_w, near, far, rows_out, gate_out, up_out, hidden_out = refs[2 * count :]
    span_r, span_p, prompts = spans
    tails = []
    base = 0
    for block in (*blocks_r, *blocks_p):
        rows = block.shape[0]
        rows_out[base : base + rows, :] = block[:, :width]
        tails.append(block[:, width:].astype(jnp.float32))
        base += rows
    total = base
    split = sum(b.shape[0] for b in blocks_r)
    tail = jnp.concatenate(tails, axis=0)
    lane = lax.broadcasted_iota(jnp.int32, tail.shape, 1)
    mine = (lane % experts == lax.axis_index("expert")) & (lane < 3 * experts)
    router = jnp.sum(jnp.where(mine, tail, 0.0), axis=1, keepdims=True)
    values = rows_out[...]
    gate = contract_last(values, gate_w[0])
    upward = contract_last(values, up_w[0])
    wide = contract_last(values, down_w[0])

    def moved(value, up):
        top, low = value[:split], value[split:]
        by_r, by_p = (split - span_r, total - split - prompts) if up else (span_r, prompts)
        return jnp.concatenate([pltpu.roll(top, by_r, 0), pltpu.roll(low, by_p, 0)], axis=0)

    sigma = jax.nn.sigmoid(gate)
    active = gate * sigma
    hidden = router * active * upward
    hidden_grad = router * moved(wide, True)
    gate_grad = (hidden_grad * upward * sigma * (1.0 + gate * (1.0 - sigma))).astype(jnp.bfloat16)
    upward_grad = (hidden_grad * active).astype(jnp.bfloat16)
    gate_out[...] = gate_grad
    up_out[...] = upward_grad
    hidden_out[...] = moved(hidden, False).astype(jnp.bfloat16)
    half = near.shape[0]
    tokens = 2 * half
    each = span_r + span_p
    slot = lax.broadcasted_iota(jnp.int32, (tokens, total), 0)
    row = lax.broadcasted_iota(jnp.int32, (tokens, total), 1)
    source, token = slot // each, slot % each
    from_r = source * (2 * span_r) + token
    n_resp = prompts // span_p
    giver = (lax.axis_index("resp") + n_resp - source % n_resp) % n_resp
    from_p = split + source // n_resp * (2 * prompts) + giver * span_p + token - span_r
    chosen = (row == jnp.where(token < span_r, from_r, from_p)).astype(jnp.float32).astype(jnp.bfloat16)
    gate_grad = jnp.dot(chosen, gate_grad, preferred_element_type=jnp.float32).astype(jnp.bfloat16)
    upward_grad = jnp.dot(chosen, upward_grad, preferred_element_type=jnp.float32).astype(jnp.bfloat16)
    step = 1024 if width % 1024 == 0 else width
    for c in range(0, width, step):
        value = jnp.dot(gate_grad, gate_w[0, :, c : c + step], preferred_element_type=jnp.float32)
        value = value + jnp.dot(upward_grad, up_w[0, :, c : c + step], preferred_element_type=jnp.float32)
        near[:, c : c + step] = value[:half].astype(jnp.bfloat16)
        far[:, c : c + step] = value[half:].astype(jnp.bfloat16)


def load_kernel(*refs):
    count = (len(refs) - 1) // 2
    arrived = refs[-1]
    copies = [pltpu.make_async_copy(refs[i], refs[count + i], arrived.at[i]) for i in range(count)]
    for copy in copies:
        copy.start()
    for copy in copies:
        copy.wait()


def outer_kernel(left, values, out, turned, buffer, sent):
    turned[...] = left[...].astype(jnp.float32).T.astype(jnp.bfloat16)
    steps = sent.shape[0]
    step = values.shape[1] // steps
    copies = []
    for c in range(steps):
        block = jnp.dot(turned[...], values[:, c * step : (c + 1) * step], preferred_element_type=jnp.float32)
        buffer[c] = block.astype(jnp.bfloat16)
        copies.append(pltpu.make_async_copy(buffer.at[c], out.at[0, :, pl.ds(c * step, step)], sent.at[c]))
        copies[-1].start()
    for copy in copies:
        copy.wait()


def outer(left, values, small):
    rows, units = left.shape
    width = values.shape[1]
    steps = 4 if width % 512 == 0 else 1
    given = [held(a, pltpu.VMEM) for a in (left, values)] if small else [left, values]
    return pl.pallas_call(
        outer_kernel,
        out_shape=(pltpu.HBM if small else jax.ShapeDtypeStruct)((1, units, width), jnp.bfloat16),
        in_specs=[VMEM] * 2,
        out_specs=HBM,
        scratch_shapes=[
            pltpu.VMEM((units, rows), jnp.bfloat16),
            pltpu.VMEM((steps, units, width // steps), jnp.bfloat16),
            pltpu.SemaphoreType.DMA((steps,)),
        ],
        compiler_params=params(24 if small else 60),
        cost_estimate=pl.CostEstimate(flops=2 * rows * units * width, bytes_accessed=2 * units * width, transcendentals=0),
        name="outer",
    )(*given)


def finish_kernel(rows_r, *refs):
    parts, prompt_out, resp_out = refs[:-2], refs[-2], refs[-1]
    total = parts[0][...].astype(jnp.float32)
    for part in parts[1:]:
        total = total + part[...].astype(jnp.float32)
    total = total.astype(jnp.bfloat16)
    responses, length = resp_out.shape[1:3]
    for i in range(responses):
        resp_out[0, i] = total[i * length : (i + 1) * length]
    prompt_out[0] = total[rows_r:]


def body(
    x_prompt,
    x_resp,
    prompt_cot,
    resp_cot,
    route_prompt,
    route_resp,
    weight_prompt,
    weight_resp,
    w_gate,
    w_up,
    w_down,
):
    n_resp = lax.axis_size("resp")
    n_expert = lax.axis_size("expert")
    chips = n_expert // 2
    experts = n_expert * w_gate.shape[0]
    hidden_units = w_gate.shape[1]
    width = x_prompt.shape[-1]
    rows_p = x_prompt.shape[1]
    rows_r = x_resp.shape[1] * x_resp.shape[2]
    bf16 = jnp.bfloat16

    given = [held(a, pltpu.HBM) for a in (x_prompt, x_resp, prompt_cot, resp_cot)]
    routing = [route_prompt, jnp.swapaxes(route_resp, -1, -2), weight_prompt, jnp.swapaxes(weight_resp, -1, -2)]
    routing = [held(a, pltpu.HBM) for a in routing]
    prompts = prompt_cot.shape[2]
    sent_r, sent_p = pl.pallas_call(
        functools.partial(prepare_kernel, experts),
        out_shape=[
            jax.ShapeDtypeStruct((2 * rows_r, width + LANES), bf16),
            jax.ShapeDtypeStruct((2 * prompts, width + LANES), bf16),
        ],
        in_specs=[HBM] * 8,
        out_specs=[VMEM] * 2,
        scratch_shapes=[pltpu.VMEM(a.shape, a.dtype) for a in given]
        + [pltpu.SMEM(a.shape, a.dtype) for a in routing]
        + [pltpu.SemaphoreType.DMA((8,))],
        compiler_params=params(8),
        name="prepare",
    )(*given, *routing)

    def spread(line):
        near = [line] + [along("expert", n_expert, 2 * j)(line) for j in range(1, chips)]
        return near + [other_core(block, n_expert) for block in near]

    weights = [w_gate, w_up, w_down]
    small = n_resp * n_expert <= 32
    if small:
        weights = pl.pallas_call(
            load_kernel,
            out_shape=[pltpu.VMEM(w.shape, w.dtype) for w in weights],
            in_specs=[HBM] * 3,
            out_specs=[VMEM] * 3,
            scratch_shapes=[pltpu.SemaphoreType.DMA((3,))],
            compiler_params=params(8),
            cost_estimate=pl.CostEstimate(flops=0, bytes_accessed=6 * w_gate.size, transcendentals=0),
            name="load",
        )(*[held(w, pltpu.HBM) for w in weights])
    by = 1
    while by < n_resp:
        if by == 2:
            sent_p, *weights = lax.optimization_barrier((sent_p, *weights))
        got = lax.ppermute(sent_p, "resp", [(i, i ^ by) for i in range(n_resp)])
        sent_p = (sent_p.astype(jnp.float32) + got.astype(jnp.float32)).astype(bf16)
        by *= 2
    line_r = jnp.concatenate([sent_r] + [along("resp", n_resp, k)(sent_r) for k in range(1, n_resp)], axis=0)
    all_r = spread(line_r)
    all_p = spread(sent_p)

    count = len(all_r)
    rows = sum(b.shape[0] for b in (*all_r, *all_p))
    tokens = rows // 2
    half = tokens // 2
    kept = pltpu.VMEM if small else jax.ShapeDtypeStruct
    taken = [*all_r, *all_p, *weights]
    if small:
        taken = [held(a, pltpu.VMEM) for a in taken]
    near, far, values, gate_grad, upward_grad, hidden = pl.pallas_call(
        functools.partial(expert_kernel, count, (rows_r, rows_p, prompts), experts),
        out_shape=[
            kept((half, width), bf16),
            kept((half, width), bf16),
            kept((rows, width), bf16),
        ]
        + [kept((rows, hidden_units), bf16)] * 3,
        in_specs=[VMEM] * (2 * count + 3),
        out_specs=[VMEM] * 6,
        compiler_params=params(24 if small else 60),
        cost_estimate=pl.CostEstimate(flops=10 * rows * width * hidden_units, bytes_accessed=20 * 2**20, transcendentals=0),
        name="expert",
    )(*taken)

    total = near.astype(jnp.float32) + other_core(far, n_expert).astype(jnp.float32)
    total = total.astype(bf16)
    total, values, gate_grad, upward_grad, hidden = lax.optimization_barrier((total, values, gate_grad, upward_grad, hidden))
    block = half // chips
    line = total[:block].astype(jnp.float32)
    for j in range(1, chips):
        line = line + along("expert", n_expert, -2 * j)(total[j * block : (j + 1) * block]).astype(jnp.float32)
    line = line.astype(bf16)
    each = rows_r + rows_p
    own = [line[:each]] + [along("resp", n_resp, -k)(line[k * each : (k + 1) * each]) for k in range(1, n_resp)]
    grad_prompt, grad_resp = pl.pallas_call(
        functools.partial(finish_kernel, rows_r),
        out_shape=[jax.ShapeDtypeStruct(x_prompt.shape, bf16), jax.ShapeDtypeStruct(x_resp.shape, bf16)],
        in_specs=[VMEM] * n_resp,
        out_specs=[VMEM] * 2,
        compiler_params=params(8),
        name="finish",
    )(*own)
    grad_gate = outer(gate_grad, values, small)
    grad_up = outer(upward_grad, values, small)
    grad_down = outer(hidden, values, small)
    return (grad_prompt, grad_resp, grad_gate, grad_up, grad_down)


def solution(mesh):
    return jax.shard_map(
        body,
        mesh=mesh,
        in_specs=(
            P(("groups", "expert"), "resp", None),
            P(("groups", "expert"), "resp", None, None),
            P(("groups", "expert"), "resp", None, None),
            P(("groups", "expert"), "resp", None, None),
            P(("groups", "expert"), "resp", None),
            P(("groups", "expert"), "resp", None, None),
            P(("groups", "expert"), "resp", None),
            P(("groups", "expert"), "resp", None, None),
            P("expert", "resp", None),
            P("expert", "resp", None),
            P("expert", "resp", None),
        ),
        out_specs=(
            P(("groups", "expert"), "resp", None),
            P(("groups", "expert"), "resp", None, None),
            P(("groups", "expert"), "resp", None),
            P(("groups", "expert"), "resp", None),
            P(("groups", "expert"), "resp", None),
        ),
        check_vma=False,
    )
```

```python
import functools

import jax
import jax.numpy as jnp
from jax import lax
from jax.experimental import pallas as pl
from jax.experimental.pallas import tpu as pltpu
from jax.sharding import PartitionSpec as P

LANES = 128
held = pltpu.with_memory_space_constraint
VMEM = pl.BlockSpec(memory_space=pltpu.VMEM)
HBM = pl.BlockSpec(memory_space=pltpu.HBM)


def params(mib):
    return pltpu.CompilerParams(vmem_limit_bytes=mib * 2**20)


def contract_last(left, right):
    return lax.dot_general(
        left, right, (((1,), (1,)), ((), ())), preferred_element_type=jnp.float32
    )


def contract_first(left, right):
    return lax.dot_general(
        left, right, (((0,), (0,)), ((), ())), preferred_element_type=jnp.float32
    )


def along(axis, size, by):
    return lambda value: lax.ppermute(value, axis, [(i, (i + by) % size) for i in range(size)])


def across(value, size, by):
    return lax.ppermute(value, "resp", [(i, i ^ by) for i in range(size)])


def other_core(value, size):
    return lax.ppermute(value, "expert", [(i, i ^ 1) for i in range(size)])


def router_row(routes, weights, row, top, experts):
    lane = lax.broadcasted_iota(jnp.int32, (1, LANES), 1)
    dense = jnp.zeros((1, LANES), jnp.float32)
    for k in range(top):
        dense = dense + jnp.where(lane % experts == routes(row, k), weights(row, k), 0.0)
    high = dense.astype(jnp.bfloat16).astype(jnp.float32)
    middle = (dense - high).astype(jnp.bfloat16).astype(jnp.float32)
    low = dense - high - middle
    part = lane // experts
    return jnp.where(part == 0, high, jnp.where(part == 1, middle, jnp.where(part == 2, low, 0.0)))


def prepare_kernel(experts, *refs):
    n_in = 8
    sources, outs, scratch = refs[:n_in], refs[n_in : len(refs) - n_in - 1], refs[len(refs) - n_in - 1 : -1]
    arrived = refs[-1]
    copies = [pltpu.make_async_copy(a, b, arrived.at[i]) for i, (a, b) in enumerate(zip(sources, scratch, strict=True))]
    for copy in copies:
        copy.start()
    for copy in copies:
        copy.wait()
    x_prompt, x_resp, prompt_cot, resp_cot, route_p, route_r, weight_p, weight_r = scratch
    sent_r, sent_p = outs
    width = x_prompt.shape[-1]
    rows_p = x_prompt.shape[1]
    responses, length = x_resp.shape[1:3]
    top = route_p.shape[-1]
    x = [x_resp[0, i].astype(jnp.float32) for i in range(responses)]
    dy = [resp_cot[0, i].astype(jnp.float32) for i in range(responses)]
    sent_r[:, :width] = jnp.concatenate(x + dy, axis=0).astype(jnp.bfloat16)
    extra = sent_r.shape[1] - width - LANES
    rows = x_prompt[0].astype(jnp.float32)
    rows = [rows[t : t + 1, c : c + extra] for t in range(rows_p) for c in range(0, width, extra)]
    sent_r[:, width : width + extra] = jnp.concatenate(rows, axis=0).astype(jnp.bfloat16)
    rows = [
        router_row(lambda t, k: route_r[0, i, k, t], lambda t, k: weight_r[0, i, k, t], t, top, experts)
        for i in range(responses)
        for t in range(length)
    ]
    rows += [
        router_row(lambda t, k: route_p[0, t, k], lambda t, k: weight_p[0, t, k], t, top, experts)
        for t in range(rows_p)
    ]
    rows.append(jnp.zeros((sent_r.shape[0] - len(rows), LANES), jnp.float32))
    sent_r[:, width + extra :] = jnp.concatenate(rows, axis=0).astype(jnp.bfloat16)
    cot = prompt_cot[0, 0].astype(jnp.float32)
    for i in range(1, responses):
        cot = cot + prompt_cot[0, i].astype(jnp.float32)
    sent_p[...] = cot.astype(jnp.bfloat16)


def expert_kernel(count, spans, experts, *refs):
    blocks_r, blocks_p = refs[:count], refs[count : 2 * count]
    gate_w, up_w, down_w, near, far, rows_out, gate_out, up_out, hidden_out = refs[2 * count :]
    span_r, span_p = spans
    width = rows_out.shape[1]
    line, prompts = blocks_r[0].shape[0], blocks_p[0].shape[0]
    n_resp = prompts // span_p
    extra = blocks_r[0].shape[1] - width - LANES
    split, count_p = count * line, count * prompts
    total = split + 2 * count_p
    me = lax.axis_index("resp")

    for i, block in enumerate(blocks_r):
        rows_out[i * line : (i + 1) * line, :] = block[:, :width]
    cot = [block[...].astype(jnp.float32) for block in blocks_p]
    rows_out[split + count_p :, :] = jnp.concatenate(cot, axis=0).astype(jnp.bfloat16)
    pieces = jnp.concatenate([block[:, width:].astype(jnp.float32) for block in blocks_r], axis=0).astype(jnp.bfloat16)
    row = lax.broadcasted_iota(jnp.int32, (count_p, split), 0)
    source = lax.broadcasted_iota(jnp.int32, (count_p, split), 1)
    of = row % prompts
    first = row // prompts * line + ((of // span_p) ^ me) * (2 * span_r)

    def picked(offset):
        return (source == first + offset).astype(jnp.float32).astype(jnp.bfloat16)

    each = width // extra
    for q in range(each):
        part = jnp.dot(picked(of % span_p * each + q), pieces[:, :extra], preferred_element_type=jnp.float32)
        rows_out[split : split + count_p, q * extra : (q + 1) * extra] = part.astype(jnp.bfloat16)

    def router_of(tail):
        lane = lax.broadcasted_iota(jnp.int32, tail.shape, 1)
        mine = (lane % experts == lax.axis_index("expert")) & (lane < 3 * experts)
        return jnp.sum(jnp.where(mine, tail, 0.0), axis=1, keepdims=True)

    tail = pieces[:, extra:]
    router_r = router_of(tail.astype(jnp.float32))
    at = lax.broadcasted_iota(jnp.int32, router_r.shape, 0)
    router_r = jnp.where(at % (2 * span_r) < span_r, router_r, 0.0)
    router_p = router_of(jnp.dot(picked(span_r + of % span_p), tail, preferred_element_type=jnp.float32))
    none = jnp.zeros((count_p, 1), jnp.float32)
    router = jnp.concatenate([router_r, router_p, none], axis=0)

    values = rows_out[...]
    gate = contract_last(values, gate_w[0])
    upward = contract_last(values, up_w[0])
    wide = contract_last(values, down_w[0])
    sigma = jax.nn.sigmoid(gate)
    active = gate * sigma
    hidden = router * active * upward
    here = split + count_p
    moved = jnp.concatenate([pltpu.roll(wide[:split], split - span_r, 0), wide[here:], wide[split:here]], axis=0)
    hidden_out[...] = jnp.concatenate(
        [pltpu.roll(hidden[:split], span_r, 0), hidden[here:], hidden[split:here]], axis=0
    ).astype(jnp.bfloat16)
    hidden_grad = router * moved
    gate_grad = (hidden_grad * upward * sigma * (1.0 + gate * (1.0 - sigma))).astype(jnp.bfloat16)
    upward_grad = (hidden_grad * active).astype(jnp.bfloat16)
    gate_out[...] = gate_grad
    up_out[...] = upward_grad
    half = near.shape[0]
    tokens = 2 * half
    span = span_r + span_p
    slot = lax.broadcasted_iota(jnp.int32, (tokens, total), 0)
    row = lax.broadcasted_iota(jnp.int32, (tokens, total), 1)
    source, token = slot // span, slot % span
    from_r = source * (2 * span_r) + token
    giver = (source % n_resp) ^ me
    from_p = split + source // n_resp * prompts + giver * span_p + token - span_r
    chosen = (row == jnp.where(token < span_r, from_r, from_p)).astype(jnp.float32).astype(jnp.bfloat16)
    gate_grad = jnp.dot(chosen, gate_grad, preferred_element_type=jnp.float32).astype(jnp.bfloat16)
    upward_grad = jnp.dot(chosen, upward_grad, preferred_element_type=jnp.float32).astype(jnp.bfloat16)
    step = 1024 if width % 1024 == 0 else width
    for c in range(0, width, step):
        value = jnp.dot(gate_grad, gate_w[0, :, c : c + step], preferred_element_type=jnp.float32)
        value = value + jnp.dot(upward_grad, up_w[0, :, c : c + step], preferred_element_type=jnp.float32)
        near[:, c : c + step] = value[:half].astype(jnp.bfloat16)
        far[:, c : c + step] = value[half:].astype(jnp.bfloat16)


def load_kernel(*refs):
    count = (len(refs) - 1) // 2
    arrived = refs[-1]
    copies = [pltpu.make_async_copy(refs[i], refs[count + i], arrived.at[i]) for i in range(count)]
    for copy in copies:
        copy.start()
    for copy in copies:
        copy.wait()


def outer_kernel(left, values, out, turned, buffer, sent):
    turned[...] = left[...].astype(jnp.float32).T.astype(jnp.bfloat16)
    steps = sent.shape[0]
    step = values.shape[1] // steps
    copies = []
    for c in range(steps):
        block = jnp.dot(turned[...], values[:, c * step : (c + 1) * step], preferred_element_type=jnp.float32)
        buffer[c] = block.astype(jnp.bfloat16)
        copies.append(pltpu.make_async_copy(buffer.at[c], out.at[0, :, pl.ds(c * step, step)], sent.at[c]))
        copies[-1].start()
    for copy in copies:
        copy.wait()


def outer(left, values, small):
    rows, units = left.shape
    width = values.shape[1]
    steps = 4 if width % 512 == 0 else 1
    given = [held(a, pltpu.VMEM) for a in (left, values)] if small else [left, values]
    return pl.pallas_call(
        outer_kernel,
        out_shape=(pltpu.HBM if small else jax.ShapeDtypeStruct)((1, units, width), jnp.bfloat16),
        in_specs=[VMEM] * 2,
        out_specs=HBM,
        scratch_shapes=[
            pltpu.VMEM((units, rows), jnp.bfloat16),
            pltpu.VMEM((steps, units, width // steps), jnp.bfloat16),
            pltpu.SemaphoreType.DMA((steps,)),
        ],
        compiler_params=params(24 if small else 60),
        cost_estimate=pl.CostEstimate(flops=2 * rows * units * width, bytes_accessed=2 * units * width, transcendentals=0),
        name="outer",
    )(*given)


def finish_kernel(rows_r, *refs):
    parts, prompt_out, resp_out = refs[:-2], refs[-2], refs[-1]
    total = parts[0][...].astype(jnp.float32)
    for part in parts[1:]:
        total = total + part[...].astype(jnp.float32)
    total = total.astype(jnp.bfloat16)
    responses, length = resp_out.shape[1:3]
    for i in range(responses):
        resp_out[0, i] = total[i * length : (i + 1) * length]
    prompt_out[0] = total[rows_r:]


def body(
    x_prompt,
    x_resp,
    prompt_cot,
    resp_cot,
    route_prompt,
    route_resp,
    weight_prompt,
    weight_resp,
    w_gate,
    w_up,
    w_down,
):
    n_resp = lax.axis_size("resp")
    n_expert = lax.axis_size("expert")
    chips = n_expert // 2
    experts = n_expert * w_gate.shape[0]
    hidden_units = w_gate.shape[1]
    width = x_prompt.shape[-1]
    rows_p = x_prompt.shape[1]
    rows_r = x_resp.shape[1] * x_resp.shape[2]
    bf16 = jnp.bfloat16

    given = [held(a, pltpu.HBM) for a in (x_prompt, x_resp, prompt_cot, resp_cot)]
    routing = [route_prompt, jnp.swapaxes(route_resp, -1, -2), weight_prompt, jnp.swapaxes(weight_resp, -1, -2)]
    routing = [held(a, pltpu.HBM) for a in routing]
    prompts = prompt_cot.shape[2]
    extra = rows_p * width // (2 * rows_r)
    sent_r, sent_p = pl.pallas_call(
        functools.partial(prepare_kernel, experts),
        out_shape=[
            jax.ShapeDtypeStruct((2 * rows_r, width + extra + LANES), bf16),
            jax.ShapeDtypeStruct((prompts, width), bf16),
        ],
        in_specs=[HBM] * 8,
        out_specs=[VMEM] * 2,
        scratch_shapes=[pltpu.VMEM(a.shape, a.dtype) for a in given]
        + [pltpu.SMEM(a.shape, a.dtype) for a in routing]
        + [pltpu.SemaphoreType.DMA((8,))],
        compiler_params=params(8),
        name="prepare",
    )(*given, *routing)

    weights = [w_gate, w_up, w_down]
    small = n_resp * n_expert <= 32
    if small:
        weights = pl.pallas_call(
            load_kernel,
            out_shape=[pltpu.VMEM(w.shape, w.dtype) for w in weights],
            in_specs=[HBM] * 3,
            out_specs=[VMEM] * 3,
            scratch_shapes=[pltpu.SemaphoreType.DMA((3,))],
            compiler_params=params(8),
            cost_estimate=pl.CostEstimate(flops=0, bytes_accessed=6 * w_gate.size, transcendentals=0),
            name="load",
        )(*[held(w, pltpu.HBM) for w in weights])
    if sent_p.shape[0] == sent_r.shape[0]:
        got = across(jnp.concatenate([sent_r, sent_p], axis=1), n_resp, 1)
        got_r, got_p = got[:, : sent_r.shape[1]], got[:, sent_r.shape[1] :]
    else:
        got_r, got_p = across(sent_r, n_resp, 1), across(sent_p, n_resp, 1)
    rest_r = [got_r] + [across(sent_r, n_resp, by) for by in range(2, n_resp)]
    by = 1
    while by < n_resp:
        got_p = got_p if by == 1 else across(sent_p, n_resp, by)
        sent_p = (sent_p.astype(jnp.float32) + got_p.astype(jnp.float32)).astype(bf16)
        if by == 1:
            sent_p, *weights = lax.optimization_barrier((sent_p, *weights))
        by *= 2
    over = [along("expert", n_expert, 2 * j) for j in range(1, chips)]
    line_r = jnp.concatenate([sent_r, *rest_r], axis=0)
    far_r = [move(line_r) for move in over]
    far_p = [move(sent_p) for move in over]
    far_r, far_p = lax.optimization_barrier((far_r, far_p))
    near_r, near_p = [line_r, *far_r], [sent_p, *far_p]
    all_r = near_r + [other_core(block, n_expert) for block in near_r]
    all_p = near_p + [other_core(block, n_expert) for block in near_p]
    count = len(all_r)
    rows = count * (line_r.shape[0] + 2 * prompts)
    tokens = rows // 2
    half = tokens // 2
    kept = pltpu.VMEM if small else jax.ShapeDtypeStruct
    taken = [*all_r, *all_p, *weights]
    if small:
        taken = [held(a, pltpu.VMEM) for a in taken]
    near, far, values, gate_grad, upward_grad, hidden = pl.pallas_call(
        functools.partial(expert_kernel, count, (rows_r, rows_p), experts),
        out_shape=[
            kept((half, width), bf16),
            kept((half, width), bf16),
            kept((rows, width), bf16),
        ]
        + [kept((rows, hidden_units), bf16)] * 3,
        in_specs=[VMEM] * (2 * count + 3),
        out_specs=[VMEM] * 6,
        compiler_params=params(24 if small else 60),
        cost_estimate=pl.CostEstimate(flops=10 * rows * width * hidden_units, bytes_accessed=20 * 2**20, transcendentals=0),
        name="expert",
    )(*taken)

    total = near.astype(jnp.float32) + other_core(far, n_expert).astype(jnp.float32)
    total = total.astype(bf16)
    total, values, gate_grad, upward_grad, hidden = lax.optimization_barrier((total, values, gate_grad, upward_grad, hidden))
    block = half // chips
    line = total[:block].astype(jnp.float32)
    for j in range(1, chips):
        line = line + along("expert", n_expert, -2 * j)(total[j * block : (j + 1) * block]).astype(jnp.float32)
    line = line.astype(bf16)
    each = rows_r + rows_p
    own = [line[:each]] + [across(line[k * each : (k + 1) * each], n_resp, k) for k in range(1, n_resp)]
    grad_prompt, grad_resp = pl.pallas_call(
        functools.partial(finish_kernel, rows_r),
        out_shape=[jax.ShapeDtypeStruct(x_prompt.shape, bf16), jax.ShapeDtypeStruct(x_resp.shape, bf16)],
        in_specs=[VMEM] * n_resp,
        out_specs=[VMEM] * 2,
        compiler_params=params(8),
        name="finish",
    )(*own)
    grad_gate = outer(gate_grad, values, small)
    grad_up = outer(upward_grad, values, small)
    grad_down = outer(hidden, values, small)
    return (grad_prompt, grad_resp, grad_gate, grad_up, grad_down)


def solution(mesh):
    return jax.shard_map(
        body,
        mesh=mesh,
        in_specs=(
            P(("groups", "expert"), "resp", None),
            P(("groups", "expert"), "resp", None, None),
            P(("groups", "expert"), "resp", None, None),
            P(("groups", "expert"), "resp", None, None),
            P(("groups", "expert"), "resp", None),
            P(("groups", "expert"), "resp", None, None),
            P(("groups", "expert"), "resp", None),
            P(("groups", "expert"), "resp", None, None),
            P("expert", "resp", None),
            P("expert", "resp", None),
            P("expert", "resp", None),
        ),
        out_specs=(
            P(("groups", "expert"), "resp", None),
            P(("groups", "expert"), "resp", None, None),
            P(("groups", "expert"), "resp", None),
            P(("groups", "expert"), "resp", None),
            P(("groups", "expert"), "resp", None),
        ),
        check_vma=False,
    )
```

```python
import functools

import jax
import jax.numpy as jnp
from jax import lax
from jax.experimental import pallas as pl
from jax.experimental.pallas import tpu as pltpu
from jax.sharding import PartitionSpec as P

LANES = 128
held = pltpu.with_memory_space_constraint
VMEM = pl.BlockSpec(memory_space=pltpu.VMEM)
HBM = pl.BlockSpec(memory_space=pltpu.HBM)


def params(mib):
    return pltpu.CompilerParams(vmem_limit_bytes=mib * 2**20)


def contract_last(left, right):
    return lax.dot_general(
        left, right, (((1,), (1,)), ((), ())), preferred_element_type=jnp.float32
    )


def contract_first(left, right):
    return lax.dot_general(
        left, right, (((0,), (0,)), ((), ())), preferred_element_type=jnp.float32
    )


def along(axis, size, by):
    return lambda value: lax.ppermute(value, axis, [(i, (i + by) % size) for i in range(size)])


def across(value, size, by):
    return lax.ppermute(value, "resp", [(i, i ^ by) for i in range(size)])


def other_core(value, size):
    return lax.ppermute(value, "expert", [(i, i ^ 1) for i in range(size)])


def router_row(routes, weights, row, top, experts):
    lane = lax.broadcasted_iota(jnp.int32, (1, LANES), 1)
    dense = jnp.zeros((1, LANES), jnp.float32)
    for k in range(top):
        dense = dense + jnp.where(lane % experts == routes(row, k), weights(row, k), 0.0)
    high = dense.astype(jnp.bfloat16).astype(jnp.float32)
    middle = (dense - high).astype(jnp.bfloat16).astype(jnp.float32)
    low = dense - high - middle
    part = lane // experts
    return jnp.where(part == 0, high, jnp.where(part == 1, middle, jnp.where(part == 2, low, 0.0)))


def prepare_kernel(experts, *refs):
    n_in = 8
    sources, outs, scratch = refs[:n_in], refs[n_in : len(refs) - n_in - 1], refs[len(refs) - n_in - 1 : -1]
    arrived = refs[-1]
    copies = [pltpu.make_async_copy(a, b, arrived.at[i]) for i, (a, b) in enumerate(zip(sources, scratch, strict=True))]
    for copy in copies:
        copy.start()
    for copy in copies:
        copy.wait()
    x_prompt, x_resp, prompt_cot, resp_cot, route_p, route_r, weight_p, weight_r = scratch
    sent_r, sent_p = outs
    width = x_prompt.shape[-1]
    rows_p = x_prompt.shape[1]
    responses, length = x_resp.shape[1:3]
    top = route_p.shape[-1]
    x = [x_resp[0, i].astype(jnp.float32) for i in range(responses)]
    dy = [resp_cot[0, i].astype(jnp.float32) for i in range(responses)]
    sent_r[:, :width] = jnp.concatenate(x + dy, axis=0).astype(jnp.bfloat16)
    extra = sent_r.shape[1] - width - LANES
    rows = x_prompt[0].astype(jnp.float32)
    rows = [rows[t : t + 1, c : c + extra] for t in range(rows_p) for c in range(0, width, extra)]
    sent_r[:, width : width + extra] = jnp.concatenate(rows, axis=0).astype(jnp.bfloat16)
    rows = [
        router_row(lambda t, k: route_r[0, i, k, t], lambda t, k: weight_r[0, i, k, t], t, top, experts)
        for i in range(responses)
        for t in range(length)
    ]
    rows += [
        router_row(lambda t, k: route_p[0, t, k], lambda t, k: weight_p[0, t, k], t, top, experts)
        for t in range(rows_p)
    ]
    rows.append(jnp.zeros((sent_r.shape[0] - len(rows), LANES), jnp.float32))
    sent_r[:, width + extra :] = jnp.concatenate(rows, axis=0).astype(jnp.bfloat16)
    cot = prompt_cot[0, 0].astype(jnp.float32)
    for i in range(1, responses):
        cot = cot + prompt_cot[0, i].astype(jnp.float32)
    sent_p[...] = cot.astype(jnp.bfloat16)


def expert_kernel(count, spans, experts, *refs):
    blocks_r, blocks_p = refs[:count], refs[count : 2 * count]
    gate_w, up_w, down_w, near, far, rows_out, gate_out, up_out, hidden_out = refs[2 * count : 2 * count + 9]
    span_r, span_p = spans
    width = rows_out.shape[1]
    line, prompts = blocks_r[0].shape[0], blocks_p[0].shape[0]
    n_resp = prompts // span_p
    extra = blocks_r[0].shape[1] - width - LANES
    split, count_p = count * line, count * prompts
    total = split + 2 * count_p
    me = lax.axis_index("resp")

    for i, block in enumerate(blocks_r):
        rows_out[i * line : (i + 1) * line, :] = block[:, :width]
    cot = [block[...].astype(jnp.float32) for block in blocks_p]
    rows_out[split + count_p :, :] = jnp.concatenate(cot, axis=0).astype(jnp.bfloat16)
    pieces = jnp.concatenate([block[:, width:].astype(jnp.float32) for block in blocks_r], axis=0).astype(jnp.bfloat16)
    row = lax.broadcasted_iota(jnp.int32, (count_p, split), 0)
    source = lax.broadcasted_iota(jnp.int32, (count_p, split), 1)
    of = row % prompts
    first = row // prompts * line + ((of // span_p) ^ me) * (2 * span_r)

    def picked(offset):
        return (source == first + offset).astype(jnp.float32).astype(jnp.bfloat16)

    each = width // extra
    for q in range(each):
        part = jnp.dot(picked(of % span_p * each + q), pieces[:, :extra], preferred_element_type=jnp.float32)
        rows_out[split : split + count_p, q * extra : (q + 1) * extra] = part.astype(jnp.bfloat16)

    def router_of(tail):
        lane = lax.broadcasted_iota(jnp.int32, tail.shape, 1)
        mine = (lane % experts == lax.axis_index("expert")) & (lane < 3 * experts)
        return jnp.sum(jnp.where(mine, tail, 0.0), axis=1, keepdims=True)

    tail = pieces[:, extra:]
    router_r = router_of(tail.astype(jnp.float32))
    at = lax.broadcasted_iota(jnp.int32, router_r.shape, 0)
    router_r = jnp.where(at % (2 * span_r) < span_r, router_r, 0.0)
    router_p = router_of(jnp.dot(picked(span_r + of % span_p), tail, preferred_element_type=jnp.float32))
    none = jnp.zeros((count_p, 1), jnp.float32)
    router = jnp.concatenate([router_r, router_p, none], axis=0)

    values = rows_out[...]
    gate = contract_last(values, gate_w[0])
    upward = contract_last(values, up_w[0])
    wide = contract_last(values, down_w[0])
    sigma = jax.nn.sigmoid(gate)
    active = gate * sigma
    hidden = router * active * upward
    here = split + count_p
    moved = jnp.concatenate([pltpu.roll(wide[:split], split - span_r, 0), wide[here:], wide[split:here]], axis=0)
    hidden_out[...] = jnp.concatenate(
        [pltpu.roll(hidden[:split], span_r, 0), hidden[here:], hidden[split:here]], axis=0
    ).astype(jnp.bfloat16)
    hidden_grad = router * moved
    gate_grad = (hidden_grad * upward * sigma * (1.0 + gate * (1.0 - sigma))).astype(jnp.bfloat16)
    upward_grad = (hidden_grad * active).astype(jnp.bfloat16)
    gate_out[...] = gate_grad
    up_out[...] = upward_grad
    packed = refs[-1] if len(refs) > 2 * count + 9 else None
    half = near.shape[0]
    sources = count * n_resp
    span = span_r + span_p
    tokens = sources * span
    slot = lax.broadcasted_iota(jnp.int32, (tokens, total), 0)
    row = lax.broadcasted_iota(jnp.int32, (tokens, total), 1)
    if packed is None:
        source, token = slot // span, slot % span
        of_prompt = token >= span_r
        prompt = token - span_r
    else:
        of_prompt = slot >= sources * span_r
        prompt = slot - sources * span_r
        source = jnp.where(of_prompt, prompt // span_p, slot // span_r)
        token, prompt = slot % span_r, prompt % span_p
    from_r = source * (2 * span_r) + token
    giver = (source % n_resp) ^ me
    from_p = split + source // n_resp * prompts + giver * span_p + prompt
    chosen = (row == jnp.where(of_prompt, from_p, from_r)).astype(jnp.float32).astype(jnp.bfloat16)
    gate_grad = jnp.dot(chosen, gate_grad, preferred_element_type=jnp.float32).astype(jnp.bfloat16)
    upward_grad = jnp.dot(chosen, upward_grad, preferred_element_type=jnp.float32).astype(jnp.bfloat16)
    for q in range(each):
        c = q * extra
        value = jnp.dot(gate_grad, gate_w[0, :, c : c + extra], preferred_element_type=jnp.float32)
        value = value + jnp.dot(upward_grad, up_w[0, :, c : c + extra], preferred_element_type=jnp.float32)
        if packed is None:
            near[:, c : c + extra] = value[:half].astype(jnp.bfloat16)
            far[:, c : c + extra] = value[half:].astype(jnp.bfloat16)
        else:
            line, at = divmod(c, width // 2)
            for i in range(0, extra, LANES):
                lanes = value[:, i : i + LANES]
                packed[(at + i) // LANES, pl.ds(line, sources * span_r, stride=2), :] = lanes[: sources * span_r]
                packed[(width // 2 + i) // LANES, pl.ds(q, sources * span_p, stride=each), :] = lanes[sources * span_r :]
    if packed is not None:
        for i in range(packed.shape[0]):
            near[:, i * LANES : (i + 1) * LANES] = packed[i, :half].astype(jnp.bfloat16)
            far[:, i * LANES : (i + 1) * LANES] = packed[i, half:].astype(jnp.bfloat16)


def load_kernel(*refs):
    count = (len(refs) - 1) // 2
    arrived = refs[-1]
    copies = [pltpu.make_async_copy(refs[i], refs[count + i], arrived.at[i]) for i in range(count)]
    for copy in copies:
        copy.start()
    for copy in copies:
        copy.wait()


def outer_kernel(left, values, out, turned, buffer, sent):
    turned[...] = left[...].astype(jnp.float32).T.astype(jnp.bfloat16)
    steps = sent.shape[0]
    step = values.shape[1] // steps
    copies = []
    for c in range(steps):
        block = jnp.dot(turned[...], values[:, c * step : (c + 1) * step], preferred_element_type=jnp.float32)
        buffer[c] = block.astype(jnp.bfloat16)
        copies.append(pltpu.make_async_copy(buffer.at[c], out.at[0, :, pl.ds(c * step, step)], sent.at[c]))
        copies[-1].start()
    for copy in copies:
        copy.wait()


def outer(left, values, small):
    rows, units = left.shape
    width = values.shape[1]
    steps = 4 if width % 512 == 0 else 1
    given = [held(a, pltpu.VMEM) for a in (left, values)] if small else [left, values]
    return pl.pallas_call(
        outer_kernel,
        out_shape=(pltpu.HBM if small else jax.ShapeDtypeStruct)((1, units, width), jnp.bfloat16),
        in_specs=[VMEM] * 2,
        out_specs=HBM,
        scratch_shapes=[
            pltpu.VMEM((units, rows), jnp.bfloat16),
            pltpu.VMEM((steps, units, width // steps), jnp.bfloat16),
            pltpu.SemaphoreType.DMA((steps,)),
        ],
        compiler_params=params(24 if small else 60),
        cost_estimate=pl.CostEstimate(flops=2 * rows * units * width, bytes_accessed=2 * units * width, transcendentals=0),
        name="outer",
    )(*given)


def finish_kernel(rows_r, rows_p, *refs):
    parts, prompt_out, resp_out = refs[: -3], refs[-3], refs[-2]
    scratch = refs[-1]
    total = parts[0][...].astype(jnp.float32)
    for part in parts[1:]:
        total = total + part[...].astype(jnp.float32)
    width = prompt_out.shape[-1]
    responses, length = resp_out.shape[1:3]
    if total.shape[1] == width:
        total = total.astype(jnp.bfloat16)
        for i in range(responses):
            resp_out[0, i] = total[i * length : (i + 1) * length]
        prompt_out[0] = total[rows_r:]
        return
    lanes, half = scratch.shape[0], width // 2 // LANES
    for i in range(lanes):
        scratch[i] = total[:, i * LANES : (i + 1) * LANES]
    rows = [scratch[i, pl.ds(line, rows_r, stride=2), :] for line in range(2) for i in range(half)]
    rows = jnp.concatenate(rows, axis=1).astype(jnp.bfloat16)
    for i in range(responses):
        resp_out[0, i] = rows[i * length : (i + 1) * length]
    each = 2 * rows_r // rows_p
    rows = [scratch[i, pl.ds(q, rows_p, stride=each), :] for q in range(each) for i in range(half, lanes)]
    prompt_out[0] = jnp.concatenate(rows, axis=1).astype(jnp.bfloat16)


def body(
    x_prompt,
    x_resp,
    prompt_cot,
    resp_cot,
    route_prompt,
    route_resp,
    weight_prompt,
    weight_resp,
    w_gate,
    w_up,
    w_down,
):
    n_resp = lax.axis_size("resp")
    n_expert = lax.axis_size("expert")
    chips = n_expert // 2
    experts = n_expert * w_gate.shape[0]
    hidden_units = w_gate.shape[1]
    width = x_prompt.shape[-1]
    rows_p = x_prompt.shape[1]
    rows_r = x_resp.shape[1] * x_resp.shape[2]
    bf16 = jnp.bfloat16

    given = [held(a, pltpu.HBM) for a in (x_prompt, x_resp, prompt_cot, resp_cot)]
    routing = [route_prompt, jnp.swapaxes(route_resp, -1, -2), weight_prompt, jnp.swapaxes(weight_resp, -1, -2)]
    routing = [held(a, pltpu.HBM) for a in routing]
    prompts = prompt_cot.shape[2]
    extra = rows_p * width // (2 * rows_r)
    sent_r, sent_p = pl.pallas_call(
        functools.partial(prepare_kernel, experts),
        out_shape=[
            jax.ShapeDtypeStruct((2 * rows_r, width + extra + LANES), bf16),
            jax.ShapeDtypeStruct((prompts, width), bf16),
        ],
        in_specs=[HBM] * 8,
        out_specs=[VMEM] * 2,
        scratch_shapes=[pltpu.VMEM(a.shape, a.dtype) for a in given]
        + [pltpu.SMEM(a.shape, a.dtype) for a in routing]
        + [pltpu.SemaphoreType.DMA((8,))],
        compiler_params=params(8),
        name="prepare",
    )(*given, *routing)

    weights = [w_gate, w_up, w_down]
    small = n_resp * n_expert <= 32
    if small:
        weights = pl.pallas_call(
            load_kernel,
            out_shape=[pltpu.VMEM(w.shape, w.dtype) for w in weights],
            in_specs=[HBM] * 3,
            out_specs=[VMEM] * 3,
            scratch_shapes=[pltpu.SemaphoreType.DMA((3,))],
            compiler_params=params(8),
            cost_estimate=pl.CostEstimate(flops=0, bytes_accessed=6 * w_gate.size, transcendentals=0),
            name="load",
        )(*[held(w, pltpu.HBM) for w in weights])
    if sent_p.shape[0] == sent_r.shape[0]:
        got = across(jnp.concatenate([sent_r, sent_p], axis=1), n_resp, 1)
        got_r, got_p = got[:, : sent_r.shape[1]], got[:, sent_r.shape[1] :]
    else:
        got_r, got_p = across(sent_r, n_resp, 1), across(sent_p, n_resp, 1)
    rest_r = [got_r] + [across(sent_r, n_resp, by) for by in range(2, n_resp)]
    by = 1
    while by < n_resp:
        got_p = got_p if by == 1 else across(sent_p, n_resp, by)
        sent_p = (sent_p.astype(jnp.float32) + got_p.astype(jnp.float32)).astype(bf16)
        if by == 1:
            sent_p, *weights = lax.optimization_barrier((sent_p, *weights))
        by *= 2
    over = [along("expert", n_expert, 2 * j) for j in range(1, chips)]
    line_r = jnp.concatenate([sent_r, *rest_r], axis=0)
    far_r = [move(line_r) for move in over]
    far_p = [move(sent_p) for move in over]
    far_r, far_p = lax.optimization_barrier((far_r, far_p))
    near_r, near_p = [line_r, *far_r], [sent_p, *far_p]
    all_r = near_r + [other_core(block, n_expert) for block in near_r]
    all_p = near_p + [other_core(block, n_expert) for block in near_p]
    count = len(all_r)
    rows = count * (line_r.shape[0] + 2 * prompts)
    tokens = rows // 2
    packed = small and 2 * rows_r % rows_p == 0 and (2 * rows_r // rows_p) % 2 == 0
    each, columns = (2 * rows_r, width // 2 + extra) if packed else (rows_r + rows_p, width)
    half = n_resp * chips * each
    kept = pltpu.VMEM if small else jax.ShapeDtypeStruct
    taken = [*all_r, *all_p, *weights]
    if small:
        taken = [held(a, pltpu.VMEM) for a in taken]
    near, far, values, gate_grad, upward_grad, hidden = pl.pallas_call(
        functools.partial(expert_kernel, count, (rows_r, rows_p), experts),
        out_shape=[
            kept((half, columns), bf16),
            kept((half, columns), bf16),
            kept((rows, width), bf16),
        ]
        + [kept((rows, hidden_units), bf16)] * 3,
        in_specs=[VMEM] * (2 * count + 3),
        out_specs=[VMEM] * 6,
        compiler_params=params(24 if small else 60),
        cost_estimate=pl.CostEstimate(flops=10 * rows * width * hidden_units, bytes_accessed=20 * 2**20, transcendentals=0),
        scratch_shapes=[pltpu.VMEM((columns // LANES, 2 * half, LANES), jnp.float32)] if packed else [],
        name="expert",
    )(*taken)

    total = near.astype(jnp.float32) + other_core(far, n_expert).astype(jnp.float32)
    total = total.astype(bf16)
    total, values, gate_grad, upward_grad, hidden = lax.optimization_barrier((total, values, gate_grad, upward_grad, hidden))
    block = half // chips
    line = total[:block].astype(jnp.float32)
    for j in range(1, chips):
        line = line + along("expert", n_expert, -2 * j)(total[j * block : (j + 1) * block]).astype(jnp.float32)
    line = line.astype(bf16)
    own = [line[:each]] + [across(line[k * each : (k + 1) * each], n_resp, k) for k in range(1, n_resp)]
    grad_prompt, grad_resp = pl.pallas_call(
        functools.partial(finish_kernel, rows_r, rows_p),
        out_shape=[jax.ShapeDtypeStruct(x_prompt.shape, bf16), jax.ShapeDtypeStruct(x_resp.shape, bf16)],
        in_specs=[VMEM] * n_resp,
        out_specs=[VMEM] * 2,
        scratch_shapes=[pltpu.VMEM((columns // LANES, each, LANES), jnp.float32)],
        compiler_params=params(8),
        name="finish",
    )(*own)
    grad_gate = outer(gate_grad, values, small)
    grad_up = outer(upward_grad, values, small)
    grad_down = outer(hidden, values, small)
    return (grad_prompt, grad_resp, grad_gate, grad_up, grad_down)


def solution(mesh):
    return jax.shard_map(
        body,
        mesh=mesh,
        in_specs=(
            P(("groups", "expert"), "resp", None),
            P(("groups", "expert"), "resp", None, None),
            P(("groups", "expert"), "resp", None, None),
            P(("groups", "expert"), "resp", None, None),
            P(("groups", "expert"), "resp", None),
            P(("groups", "expert"), "resp", None, None),
            P(("groups", "expert"), "resp", None),
            P(("groups", "expert"), "resp", None, None),
            P("expert", "resp", None),
            P("expert", "resp", None),
            P("expert", "resp", None),
        ),
        out_specs=(
            P(("groups", "expert"), "resp", None),
            P(("groups", "expert"), "resp", None, None),
            P(("groups", "expert"), "resp", None),
            P(("groups", "expert"), "resp", None),
            P(("groups", "expert"), "resp", None),
        ),
        check_vma=False,
    )
```

```python
import functools

import jax
import jax.numpy as jnp
from jax import lax
from jax.experimental import pallas as pl
from jax.experimental.pallas import tpu as pltpu
from jax.sharding import PartitionSpec as P

LANES = 128
held = pltpu.with_memory_space_constraint
VMEM = pl.BlockSpec(memory_space=pltpu.VMEM)
HBM = pl.BlockSpec(memory_space=pltpu.HBM)


def params(mib):
    return pltpu.CompilerParams(vmem_limit_bytes=mib * 2**20)


def contract_last(left, right):
    return lax.dot_general(
        left, right, (((1,), (1,)), ((), ())), preferred_element_type=jnp.float32
    )


def contract_first(left, right):
    return lax.dot_general(
        left, right, (((0,), (0,)), ((), ())), preferred_element_type=jnp.float32
    )


def along(axis, size, by):
    return lambda value: lax.ppermute(value, axis, [(i, (i + by) % size) for i in range(size)])


def across(value, size, by):
    return lax.ppermute(value, "resp", [(i, i ^ by) for i in range(size)])


def other_core(value, size):
    return lax.ppermute(value, "expert", [(i, i ^ 1) for i in range(size)])


def router_row(routes, weights, row, top, experts):
    lane = lax.broadcasted_iota(jnp.int32, (1, LANES), 1)
    dense = jnp.zeros((1, LANES), jnp.float32)
    for k in range(top):
        dense = dense + jnp.where(lane % experts == routes(row, k), weights(row, k), 0.0)
    high = dense.astype(jnp.bfloat16).astype(jnp.float32)
    middle = (dense - high).astype(jnp.bfloat16).astype(jnp.float32)
    low = dense - high - middle
    part = lane // experts
    return jnp.where(part == 0, high, jnp.where(part == 1, middle, jnp.where(part == 2, low, 0.0)))


def prepare_kernel(experts, *refs):
    n_in = 8
    sources, outs, scratch = refs[:n_in], refs[n_in : len(refs) - n_in - 1], refs[len(refs) - n_in - 1 : -1]
    arrived = refs[-1]
    copies = [pltpu.make_async_copy(a, b, arrived.at[i]) for i, (a, b) in enumerate(zip(sources, scratch, strict=True))]
    for copy in copies:
        copy.start()
    for copy in copies:
        copy.wait()
    x_prompt, x_resp, prompt_cot, resp_cot, route_p, route_r, weight_p, weight_r = scratch
    sent_r, sent_p = outs
    width = x_prompt.shape[-1]
    rows_p = x_prompt.shape[1]
    responses, length = x_resp.shape[1:3]
    top = route_p.shape[-1]
    x = [x_resp[0, i].astype(jnp.float32) for i in range(responses)]
    dy = [resp_cot[0, i].astype(jnp.float32) for i in range(responses)]
    sent_r[:, :width] = jnp.concatenate(x + dy, axis=0).astype(jnp.bfloat16)
    extra = sent_r.shape[1] - width - LANES
    rows = x_prompt[0].astype(jnp.float32)
    rows = [rows[t : t + 1, c : c + extra] for t in range(rows_p) for c in range(0, width, extra)]
    sent_r[:, width : width + extra] = jnp.concatenate(rows, axis=0).astype(jnp.bfloat16)
    rows = [
        router_row(lambda t, k: route_r[0, i, k, t], lambda t, k: weight_r[0, i, k, t], t, top, experts)
        for i in range(responses)
        for t in range(length)
    ]
    rows += [
        router_row(lambda t, k: route_p[0, t, k], lambda t, k: weight_p[0, t, k], t, top, experts)
        for t in range(rows_p)
    ]
    rows.append(jnp.zeros((sent_r.shape[0] - len(rows), LANES), jnp.float32))
    sent_r[:, width + extra :] = jnp.concatenate(rows, axis=0).astype(jnp.bfloat16)
    cot = prompt_cot[0, 0].astype(jnp.float32)
    for i in range(1, responses):
        cot = cot + prompt_cot[0, i].astype(jnp.float32)
    sent_p[...] = cot.astype(jnp.bfloat16)


def expert_kernel(count, spans, experts, *refs):
    blocks_r, blocks_p = refs[:count], refs[count : 2 * count]
    gate_w, up_w, down_w, near, far, rows_out, gate_out, up_out, hidden_out = refs[2 * count : 2 * count + 9]
    span_r, span_p = spans
    width = rows_out.shape[1]
    line, prompts = blocks_r[0].shape[0], blocks_p[0].shape[0]
    n_resp = prompts // span_p
    extra = blocks_r[0].shape[1] - width - LANES
    split, count_p = count * line, count * prompts
    total = split + 2 * count_p
    me = lax.axis_index("resp")

    for i, block in enumerate(blocks_r):
        rows_out[i * line : (i + 1) * line, :] = block[:, :width]
    cot = [block[...].astype(jnp.float32) for block in blocks_p]
    rows_out[split + count_p :, :] = jnp.concatenate(cot, axis=0).astype(jnp.bfloat16)
    pieces = jnp.concatenate([block[:, width:].astype(jnp.float32) for block in blocks_r], axis=0).astype(jnp.bfloat16)
    row = lax.broadcasted_iota(jnp.int32, (count_p, split), 0)
    source = lax.broadcasted_iota(jnp.int32, (count_p, split), 1)
    of = row % prompts
    first = row // prompts * line + ((of // span_p) ^ me) * (2 * span_r)

    def picked(offset):
        return (source == first + offset).astype(jnp.float32).astype(jnp.bfloat16)

    each = width // extra
    for q in range(each):
        part = jnp.dot(picked(of % span_p * each + q), pieces[:, :extra], preferred_element_type=jnp.float32)
        rows_out[split : split + count_p, q * extra : (q + 1) * extra] = part.astype(jnp.bfloat16)

    def router_of(tail):
        lane = lax.broadcasted_iota(jnp.int32, tail.shape, 1)
        mine = (lane % experts == lax.axis_index("expert")) & (lane < 3 * experts)
        return jnp.sum(jnp.where(mine, tail, 0.0), axis=1, keepdims=True)

    tail = pieces[:, extra:]
    router_r = router_of(tail.astype(jnp.float32))
    at = lax.broadcasted_iota(jnp.int32, router_r.shape, 0)
    router_r = jnp.where(at % (2 * span_r) < span_r, router_r, 0.0)
    router_p = router_of(jnp.dot(picked(span_r + of % span_p), tail, preferred_element_type=jnp.float32))
    none = jnp.zeros((count_p, 1), jnp.float32)
    router = jnp.concatenate([router_r, router_p, none], axis=0)

    values = rows_out[...]
    gate = contract_last(values, gate_w[0])
    upward = contract_last(values, up_w[0])
    wide = contract_last(values, down_w[0])
    sigma = jax.nn.sigmoid(gate)
    active = gate * sigma
    hidden = router * active * upward
    here = split + count_p
    moved = jnp.concatenate([pltpu.roll(wide[:split], split - span_r, 0), wide[here:], wide[split:here]], axis=0)
    hidden_out[...] = jnp.concatenate(
        [pltpu.roll(hidden[:split], span_r, 0), hidden[here:], hidden[split:here]], axis=0
    ).astype(jnp.bfloat16)
    hidden_grad = router * moved
    gate_grad = (hidden_grad * upward * sigma * (1.0 + gate * (1.0 - sigma))).astype(jnp.bfloat16)
    upward_grad = (hidden_grad * active).astype(jnp.bfloat16)
    gate_out[...] = gate_grad
    up_out[...] = upward_grad
    packed = refs[-1] if len(refs) > 2 * count + 9 else None
    half = near.shape[0]
    sources = count * n_resp
    span = span_r + span_p
    tokens = sources * span
    slot = lax.broadcasted_iota(jnp.int32, (tokens, total), 0)
    row = lax.broadcasted_iota(jnp.int32, (tokens, total), 1)
    if packed is None:
        source, token = slot // span, slot % span
        of_prompt = token >= span_r
        prompt = token - span_r
    else:
        of_prompt = slot >= sources * span_r
        prompt = slot - sources * span_r
        source = jnp.where(of_prompt, prompt // span_p, slot // span_r)
        token, prompt = slot % span_r, prompt % span_p
    from_r = source * (2 * span_r) + token
    giver = (source % n_resp) ^ me
    from_p = split + source // n_resp * prompts + giver * span_p + prompt
    chosen = (row == jnp.where(of_prompt, from_p, from_r)).astype(jnp.float32).astype(jnp.bfloat16)
    gate_grad = jnp.dot(chosen, gate_grad, preferred_element_type=jnp.float32).astype(jnp.bfloat16)
    upward_grad = jnp.dot(chosen, upward_grad, preferred_element_type=jnp.float32).astype(jnp.bfloat16)
    for q in range(each):
        c = q * extra
        value = jnp.dot(gate_grad, gate_w[0, :, c : c + extra], preferred_element_type=jnp.float32)
        value = value + jnp.dot(upward_grad, up_w[0, :, c : c + extra], preferred_element_type=jnp.float32)
        if packed is None:
            near[:, c : c + extra] = value[:half].astype(jnp.bfloat16)
            far[:, c : c + extra] = value[half:].astype(jnp.bfloat16)
        else:
            line, at = divmod(c, width // 2)
            for i in range(0, extra, LANES):
                lanes = value[:, i : i + LANES]
                packed[(at + i) // LANES, pl.ds(line, sources * span_r, stride=2), :] = lanes[: sources * span_r]
                packed[(width // 2 + i) // LANES, pl.ds(q, sources * span_p, stride=each), :] = lanes[sources * span_r :]
    if packed is not None:
        for i in range(packed.shape[0]):
            near[:, i * LANES : (i + 1) * LANES] = packed[i, :half].astype(jnp.bfloat16)
            far[:, i * LANES : (i + 1) * LANES] = packed[i, half:].astype(jnp.bfloat16)


def load_kernel(*refs):
    count = (len(refs) - 1) // 2
    arrived = refs[-1]
    copies = [pltpu.make_async_copy(refs[i], refs[count + i], arrived.at[i]) for i in range(count)]
    for copy in copies:
        copy.start()
    for copy in copies:
        copy.wait()


def outer_kernel(*refs):
    count = (len(refs) - 4) // 2
    lefts, values, outs = refs[:count], refs[count], refs[count + 1 : 2 * count + 1]
    turned, buffer, sent = refs[2 * count + 1 :]
    steps = sent.shape[1]
    step = values.shape[1] // steps
    copies = []
    for i, (left, out) in enumerate(zip(lefts, outs, strict=True)):
        turned[i] = left[...].astype(jnp.float32).T.astype(jnp.bfloat16)
        for c in range(steps):
            block = jnp.dot(turned[i], values[:, c * step : (c + 1) * step], preferred_element_type=jnp.float32)
            buffer[i, c] = block.astype(jnp.bfloat16)
            copies.append(pltpu.make_async_copy(buffer.at[i, c], out.at[0, :, pl.ds(c * step, step)], sent.at[i, c]))
            copies[-1].start()
    for copy in copies:
        copy.wait()


def outer(lefts, values, small):
    rows, units = lefts[0].shape
    width = values.shape[1]
    count = len(lefts)
    steps = 4 if width % 512 == 0 else 1
    given = [held(a, pltpu.VMEM) for a in (*lefts, values)] if small else [*lefts, values]
    return pl.pallas_call(
        outer_kernel,
        out_shape=[(pltpu.HBM if small else jax.ShapeDtypeStruct)((1, units, width), jnp.bfloat16)] * count,
        in_specs=[VMEM] * (count + 1),
        out_specs=[HBM] * count,
        scratch_shapes=[
            pltpu.VMEM((count, units, rows), jnp.bfloat16),
            pltpu.VMEM((count, steps, units, width // steps), jnp.bfloat16),
            pltpu.SemaphoreType.DMA((count, steps)),
        ],
        compiler_params=params(24 if small else 60),
        cost_estimate=pl.CostEstimate(
            flops=2 * count * rows * units * width, bytes_accessed=2 * count * units * width, transcendentals=0
        ),
        name="outer",
    )(*given)


def finish_kernel(rows_r, rows_p, *refs):
    parts, prompt_out, resp_out = refs[: -3], refs[-3], refs[-2]
    scratch = refs[-1]
    total = parts[0][...].astype(jnp.float32)
    for part in parts[1:]:
        total = total + part[...].astype(jnp.float32)
    width = prompt_out.shape[-1]
    responses, length = resp_out.shape[1:3]
    if total.shape[1] == width:
        total = total.astype(jnp.bfloat16)
        for i in range(responses):
            resp_out[0, i] = total[i * length : (i + 1) * length]
        prompt_out[0] = total[rows_r:]
        return
    lanes, half = scratch.shape[0], width // 2 // LANES
    for i in range(lanes):
        scratch[i] = total[:, i * LANES : (i + 1) * LANES]
    rows = [scratch[i, pl.ds(line, rows_r, stride=2), :] for line in range(2) for i in range(half)]
    rows = jnp.concatenate(rows, axis=1).astype(jnp.bfloat16)
    for i in range(responses):
        resp_out[0, i] = rows[i * length : (i + 1) * length]
    each = 2 * rows_r // rows_p
    rows = [scratch[i, pl.ds(q, rows_p, stride=each), :] for q in range(each) for i in range(half, lanes)]
    prompt_out[0] = jnp.concatenate(rows, axis=1).astype(jnp.bfloat16)


def body(
    x_prompt,
    x_resp,
    prompt_cot,
    resp_cot,
    route_prompt,
    route_resp,
    weight_prompt,
    weight_resp,
    w_gate,
    w_up,
    w_down,
):
    n_resp = lax.axis_size("resp")
    n_expert = lax.axis_size("expert")
    chips = n_expert // 2
    experts = n_expert * w_gate.shape[0]
    hidden_units = w_gate.shape[1]
    width = x_prompt.shape[-1]
    rows_p = x_prompt.shape[1]
    rows_r = x_resp.shape[1] * x_resp.shape[2]
    bf16 = jnp.bfloat16

    given = [held(a, pltpu.HBM) for a in (x_prompt, x_resp, prompt_cot, resp_cot)]
    routing = [route_prompt, jnp.swapaxes(route_resp, -1, -2), weight_prompt, jnp.swapaxes(weight_resp, -1, -2)]
    routing = [held(a, pltpu.HBM) for a in routing]
    prompts = prompt_cot.shape[2]
    extra = rows_p * width // (2 * rows_r)
    sent_r, sent_p = pl.pallas_call(
        functools.partial(prepare_kernel, experts),
        out_shape=[
            jax.ShapeDtypeStruct((2 * rows_r, width + extra + LANES), bf16),
            jax.ShapeDtypeStruct((prompts, width), bf16),
        ],
        in_specs=[HBM] * 8,
        out_specs=[VMEM] * 2,
        scratch_shapes=[pltpu.VMEM(a.shape, a.dtype) for a in given]
        + [pltpu.SMEM(a.shape, a.dtype) for a in routing]
        + [pltpu.SemaphoreType.DMA((8,))],
        compiler_params=params(8),
        name="prepare",
    )(*given, *routing)

    weights = [w_gate, w_up, w_down]
    small = n_resp * n_expert <= 32
    if small:
        weights = pl.pallas_call(
            load_kernel,
            out_shape=[pltpu.VMEM(w.shape, w.dtype) for w in weights],
            in_specs=[HBM] * 3,
            out_specs=[VMEM] * 3,
            scratch_shapes=[pltpu.SemaphoreType.DMA((3,))],
            compiler_params=params(8),
            cost_estimate=pl.CostEstimate(flops=0, bytes_accessed=6 * w_gate.size, transcendentals=0),
            name="load",
        )(*[held(w, pltpu.HBM) for w in weights])
    if sent_p.shape[0] == sent_r.shape[0]:
        got = across(jnp.concatenate([sent_r, sent_p], axis=1), n_resp, 1)
        got_r, got_p = got[:, : sent_r.shape[1]], got[:, sent_r.shape[1] :]
    else:
        got_r, got_p = across(sent_r, n_resp, 1), across(sent_p, n_resp, 1)
    rest_r = [got_r] + [across(sent_r, n_resp, by) for by in range(2, n_resp)]
    by = 1
    while by < n_resp:
        got_p = got_p if by == 1 else across(sent_p, n_resp, by)
        sent_p = (sent_p.astype(jnp.float32) + got_p.astype(jnp.float32)).astype(bf16)
        if by == 1:
            sent_p, *weights = lax.optimization_barrier((sent_p, *weights))
        by *= 2
    over = [along("expert", n_expert, 2 * j) for j in range(1, chips)]
    line_r = jnp.concatenate([sent_r, *rest_r], axis=0)
    far_r = [move(line_r) for move in over]
    far_p = [move(sent_p) for move in over]
    far_r, far_p = lax.optimization_barrier((far_r, far_p))
    near_r, near_p = [line_r, *far_r], [sent_p, *far_p]
    all_r = near_r + [other_core(block, n_expert) for block in near_r]
    all_p = near_p + [other_core(block, n_expert) for block in near_p]
    count = len(all_r)
    rows = count * (line_r.shape[0] + 2 * prompts)
    tokens = rows // 2
    packed = small and 2 * rows_r % rows_p == 0 and (2 * rows_r // rows_p) % 2 == 0
    each, columns = (2 * rows_r, width // 2 + extra) if packed else (rows_r + rows_p, width)
    half = n_resp * chips * each
    kept = pltpu.VMEM if small else jax.ShapeDtypeStruct
    taken = [*all_r, *all_p, *weights]
    if small:
        taken = [held(a, pltpu.VMEM) for a in taken]
    near, far, values, gate_grad, upward_grad, hidden = pl.pallas_call(
        functools.partial(expert_kernel, count, (rows_r, rows_p), experts),
        out_shape=[
            kept((half, columns), bf16),
            kept((half, columns), bf16),
            kept((rows, width), bf16),
        ]
        + [kept((rows, hidden_units), bf16)] * 3,
        in_specs=[VMEM] * (2 * count + 3),
        out_specs=[VMEM] * 6,
        compiler_params=params(24 if small else 60),
        cost_estimate=pl.CostEstimate(flops=10 * rows * width * hidden_units, bytes_accessed=20 * 2**20, transcendentals=0),
        scratch_shapes=[pltpu.VMEM((columns // LANES, 2 * half, LANES), jnp.float32)] if packed else [],
        name="expert",
    )(*taken)

    total = near.astype(jnp.float32) + other_core(far, n_expert).astype(jnp.float32)
    total = total.astype(bf16)
    total, values, gate_grad, upward_grad, hidden = lax.optimization_barrier((total, values, gate_grad, upward_grad, hidden))
    block = half // chips
    line = total[:block].astype(jnp.float32)
    for j in range(1, chips):
        line = line + along("expert", n_expert, -2 * j)(total[j * block : (j + 1) * block]).astype(jnp.float32)
    line = line.astype(bf16)
    own = [line[:each]] + [across(line[k * each : (k + 1) * each], n_resp, k) for k in range(1, n_resp)]
    grad_prompt, grad_resp = pl.pallas_call(
        functools.partial(finish_kernel, rows_r, rows_p),
        out_shape=[jax.ShapeDtypeStruct(x_prompt.shape, bf16), jax.ShapeDtypeStruct(x_resp.shape, bf16)],
        in_specs=[VMEM] * n_resp,
        out_specs=[VMEM] * 2,
        scratch_shapes=[pltpu.VMEM((columns // LANES, each, LANES), jnp.float32)],
        compiler_params=params(8),
        name="finish",
    )(*own)
    grad_gate, grad_up = outer([gate_grad, upward_grad], values, small)
    (grad_down,) = outer([hidden], values, small)
    return (grad_prompt, grad_resp, grad_gate, grad_up, grad_down)


def solution(mesh):
    return jax.shard_map(
        body,
        mesh=mesh,
        in_specs=(
            P(("groups", "expert"), "resp", None),
            P(("groups", "expert"), "resp", None, None),
            P(("groups", "expert"), "resp", None, None),
            P(("groups", "expert"), "resp", None, None),
            P(("groups", "expert"), "resp", None),
            P(("groups", "expert"), "resp", None, None),
            P(("groups", "expert"), "resp", None),
            P(("groups", "expert"), "resp", None, None),
            P("expert", "resp", None),
            P("expert", "resp", None),
            P("expert", "resp", None),
        ),
        out_specs=(
            P(("groups", "expert"), "resp", None),
            P(("groups", "expert"), "resp", None, None),
            P(("groups", "expert"), "resp", None),
            P(("groups", "expert"), "resp", None),
            P(("groups", "expert"), "resp", None),
        ),
        check_vma=False,
    )
```
